128 devices in a mesh: slab: 16 (over x, y), coil: 8 (over z, core).
Axes of the slice: x: 4, y: 4, z: 4, core: 2. Of those that a mesh axis runs over, the one named last changes fastest.
Arguments:
- samples: bfloat16 [8, 131072, 128], P('coil', 'slab'), may hold values from -6 to 6
- sample_pos: bfloat16 [131072, 64], P('slab'), may hold values from 0 to 64
- block_count: int32 [131072], P('slab'), may hold values from 16 to 64
- grid_block: int32 [131072], P('slab'), may hold values from 0 to 16383
- block_slab: int32 [131072, 1], P('slab'), may hold values from 0 to 15, as said below
- sensitivity: bfloat16 [8, 256, 16, 512], P(None, 'slab', 'coil'), may hold values from -3 to 3
Outputs:
- image: float32 [256, 16, 512], P('slab', 'coil')
The draws below stay inside these ranges and needn't reach their ends.
Inputs may be any that keep to these rules, and one draw needn't show every extreme that they name: `block_slab`: within the rows of one device no slab is named more than 1280 times; one slab, the same for every device, is named exactly 1280 times by every device.
All inputs are finite; a program needn't handle non-finite values.
Results may differ from the reference program's by a relative error of at most 0.02.
The reference program's roundings to bfloat16 on the way count: a program that leaves them out, or rounds other values in their place, can miss the bound.
Values may be sent and summed in bfloat16 or wider, within the bound.
No kernel may reach another device: no remote copies, remote signals or barrier semaphores. Data moves between devices by JAX's collectives and lax.ppermute only.
A program may use at most 128 MiB of HBM per device.

```python
import math
import jax
import jax.numpy as jnp
from jax import lax

COILS = 8
KX = 256
KY = 256
Z = 256
BLOCK_LEN = 64
XW = 16
BLK_DEV = 8192
ZP = 16
BLOCKS = 131072
CAP = 1280
NGB = 16384


def draw_block_slab(key, part):
    slab_total = BLOCKS // BLK_DEV
    remaining = BLK_DEV - CAP
    key_busy, key_share, key_order = jax.random.split(key, 3)
    busiest = jax.random.randint(key_busy, (), 0, slab_total)
    row_index = jnp.arange(BLK_DEV, dtype=jnp.int32)
    beyond = jnp.maximum(row_index - CAP, 0)

    def one_device(share_key, order_key):
        shares = jax.random.randint(share_key, (slab_total - 1,), 1, 3)
        bounds = remaining * jnp.cumsum(shares) // jnp.sum(shares)
        other_slab = 1 + jnp.sum((bounds[None, :] <= beyond[:, None]).astype(jnp.int32), axis=1)
        offset_row = jnp.where(row_index < CAP, 0, other_slab)
        slab_of = (busiest + offset_row) % slab_total
        return slab_of[jax.random.permutation(order_key, BLK_DEV)]
    drawn = jax.vmap(one_device)(jax.random.split(key_share, slab_total), jax.random.split(key_order, slab_total))
    return drawn.reshape(BLOCKS, 1).astype(jnp.int32)


def set_ends(values, key, smallest, largest):
    spot = [jax.random.randint(jax.random.fold_in(key, axis), (), 0, length) for axis, length in enumerate(values.shape)]
    widest = values.shape.index(max(values.shape))
    beside = spot[:widest] + [(spot[widest] + 1) % values.shape[widest]] + spot[widest + 1:]
    return values.at[tuple(spot)].set(smallest).at[tuple(beside)].set(largest)


def level_of(key, dims, cuts, low, high):
    def one(dim, blocks):
        steps = jax.random.uniform(jax.random.fold_in(jax.random.fold_in(key, 6), dim), (blocks,), jnp.float32, low / len(cuts), high / len(cuts))
        return jnp.repeat(jnp.exp(steps), dims[dim] // blocks).reshape((-1,) + (1,) * (len(dims) - dim - 1))

    loudness = one(*cuts[0])
    for cut in cuts[1:]:
        loudness = loudness * one(*cut)
    return loudness


def centred(key, dims, deviation, most, cuts=(), kind=jnp.bfloat16):
    values = deviation * jax.random.normal(key, dims, jnp.float32)
    if cuts:
        values = values * level_of(key, dims, cuts, -0.22, 0.18)
    return jnp.clip(values, -most, most).astype(kind)


def setup_inputs(seed: int = 0) -> dict:
    keys = jax.random.split(jax.random.key(seed), 7)
    return {
        "samples": centred(keys[0], (COILS, BLOCKS, 2 * BLOCK_LEN), 1.0, 6.0, ((0, 8), (1, 16))),
        "sample_pos": jnp.clip(64.0 * jax.random.uniform(keys[1], (BLOCKS, BLOCK_LEN), jnp.float32) ** level_of(keys[1], (BLOCKS, BLOCK_LEN), ((0, 16),), -0.2, 0.2), 0.0, 64.0).astype(jnp.bfloat16),
        "block_count": set_ends(jax.random.randint(keys[2], (BLOCKS,), 16, BLOCK_LEN + 1), jax.random.fold_in(keys[2], 1), 16, BLOCK_LEN).astype(jnp.int32),
        "grid_block": set_ends(jax.random.randint(keys[3], (BLOCKS,), 0, NGB), jax.random.fold_in(keys[3], 1), 0, NGB - 1).astype(jnp.int32),
        "block_slab": draw_block_slab(jax.random.fold_in(keys[6], 71), 0),
        "sensitivity": centred(keys[5], (COILS, Z, XW, 2 * KY), 0.5, 3.0, ((1, 16), (2, 8))),
    }


kernel_half = 2.5

def block_weights(positions, counts):
    cell_mid = jnp.arange(positions.shape[-1], dtype=jnp.int32).astype(jnp.float32) + 0.5
    offset = (positions.astype(jnp.float32)[..., :, None] - cell_mid) / kernel_half
    bump = jnp.maximum(1.0 - offset * offset, 0.0)
    live = jnp.arange(positions.shape[-1], dtype=jnp.int32)[:, None] < counts[..., None, None]
    return jnp.where(live, bump * bump, 0.0).astype(jnp.bfloat16)

def twiddle(first, second, length):
    phase = (first * second % length).astype(jnp.float32) * (2.0 * math.pi / length)
    scale = 1.0 / math.sqrt(length)
    return (jnp.cos(phase) * scale, jnp.sin(phase) * scale)

def choose(part_in, part_out, cosine, sine):
    upper = jnp.where(part_out == 0, cosine, sine)
    lower = jnp.where(part_out == 0, -sine, cosine)
    return jnp.where(part_in == 0, upper, lower).astype(jnp.bfloat16)

def across_table(kx_len, rows_out):
    index_in = jnp.arange(2 * kx_len, dtype=jnp.int32)
    segment = index_in // 128
    part_in = index_in // 64 % 2
    cell_at = segment * 64 + index_in % 64
    index_out = jnp.arange(2 * rows_out, dtype=jnp.int32)
    part_out = index_out // rows_out
    row_at = (kx_len - rows_out) // 2 + index_out % rows_out
    cosine, sine = twiddle(cell_at[:, None], row_at[None, :], kx_len)
    return choose(part_in[:, None], part_out[None, :], cosine, sine)

def square_table(length):
    index_in = jnp.arange(2 * length, dtype=jnp.int32)
    index_out = jnp.arange(2 * length, dtype=jnp.int32)
    cosine, sine = twiddle((index_in // 2)[:, None], (index_out % length)[None, :], length)
    return choose((index_in % 2)[:, None], (index_out // length)[None, :], cosine, sine)

def depth_table(positions, freqs, length):
    cosine, sine = twiddle(positions[:, None], freqs[None, :], length)
    upper = jnp.stack([cosine, -sine], axis=-1)
    lower = jnp.stack([sine, cosine], axis=-1)
    return jnp.stack([upper, lower], axis=1).astype(jnp.bfloat16)

def conj_term(coil_map, coil_image, half):
    map_re = coil_map[..., :half].astype(jnp.float32)
    map_im = coil_map[..., half:].astype(jnp.float32)
    img_re = coil_image[..., :half].astype(jnp.float32)
    img_im = coil_image[..., half:].astype(jnp.float32)
    return jnp.concatenate([map_re * img_re + map_im * img_im, map_re * img_im - map_im * img_re], axis=-1)

def reference(samples, sample_pos, block_count, grid_block, block_slab, sensitivity):
    seg_count = KX // 64
    target = (block_slab[:, 0] * (ZP * KY * seg_count) + grid_block).astype(jnp.int32)
    group_len = math.gcd(BLOCKS, 4096)
    group_count = BLOCKS // group_len

    def one_group(pieces):
        values, positions, counts = pieces
        weights = lax.optimization_barrier(block_weights(positions, counts)).astype(jnp.float32)
        shaped = values.astype(jnp.float32).reshape(COILS, group_len, 2, 64)
        result = jnp.einsum('mij,cmpi->cmpj', weights, shaped, precision=lax.Precision.HIGHEST)
        return result.reshape(COILS, group_len, 128).astype(jnp.bfloat16)
    grouped = (jnp.transpose(samples.reshape(COILS, group_count, group_len, 128), (1, 0, 2, 3)), sample_pos.reshape(group_count, group_len, 64), block_count.reshape(group_count, group_len))
    gridded = jnp.transpose(lax.map(one_group, grouped), (1, 0, 2, 3)).reshape(COILS, BLOCKS, 128)
    across = across_table(KX, XW)
    y_table = square_table(KY).reshape(KY, 2, 2 * KY).astype(jnp.float32)
    every_z = jnp.arange(Z, dtype=jnp.int32)
    depth_tab = depth_table(every_z, every_z, Z).astype(jnp.float32)

    def one_coil(running, pieces):
        cell_rows, coil_map = pieces
        cell_wide = lax.optimization_barrier(cell_rows).astype(jnp.float32)
        kspace = jnp.zeros((Z * KY * seg_count, 128), jnp.float32).at[target].add(cell_wide).astype(jnp.bfloat16)
        x_rows = jnp.dot(kspace.reshape(Z * KY, 2 * KX), across, preferred_element_type=jnp.float32).astype(jnp.bfloat16)
        x_rows = lax.optimization_barrier(x_rows).astype(jnp.float32).reshape(Z, KY, 2, XW)
        y_planes = jnp.einsum('zkqx,kqn->zxn', x_rows, y_table, precision=lax.Precision.HIGHEST).astype(jnp.bfloat16)
        y_planes = lax.optimization_barrier(y_planes).astype(jnp.float32).reshape(Z, XW, 2, KY)
        coil_image = jnp.einsum('zpkq,kxqy->zxpy', depth_tab, y_planes, precision=lax.Precision.HIGHEST)
        coil_image = coil_image.reshape(Z, XW, 2 * KY).astype(jnp.bfloat16)
        return (running + conj_term(coil_map, coil_image, KY), None)
    start_sum = jnp.zeros((Z, XW, 2 * KY), jnp.float32)
    image, _ = lax.scan(one_coil, start_sum, (gridded, sensitivity))
    return image
```

```python
import functools
import math

import jax
import jax.numpy as jnp
import numpy as np
from jax import lax
from jax.experimental import pallas as pl
from jax.experimental.pallas import tpu as pltpu
from jax.sharding import PartitionSpec as P

KX = 256
KY = 256
Z = 256
XW = 16
CELLS = 64
STEP = 512
GATHER = 2048
NT = (((1,), (1,)), ((), ()))


def twiddle(first, second, length):
    phase = (first * second % length).astype(np.float32) * np.float32(2.0 * math.pi / length)
    scale = 1.0 / math.sqrt(length)
    return np.cos(phase) * scale, np.sin(phase) * scale


def across_table():
    cell = np.arange(CELLS)
    rows = (KX - XW) // 2 + np.arange(XW)
    table = np.zeros((KX // CELLS, XW, 2, 2, 2, CELLS), np.float32)
    for s in range(KX // CELLS):
        cosine, sine = twiddle((s * CELLS + cell)[None, :], rows[:, None], KX)
        table[s, :, 0, 0] = cosine[:, None, :]
        table[s, :, 1, 0] = sine[:, None, :]
        table[s, :, 0, 1] = -sine[:, None, :]
        table[s, :, 1, 1] = cosine[:, None, :]
    return table.reshape(KX // CELLS * XW * 2, 4 * CELLS)


def line_table(length):
    index = np.arange(length)
    cosine, sine = twiddle(index[:, None], index[None, :], length)
    return np.block([[cosine, -sine], [sine, cosine]])


def depth_tables(length):
    index = np.arange(length)
    cosine, sine = twiddle(index[:, None], index[None, :], length)
    return np.stack([cosine, sine, -sine])


def grid_kernel(pos_ref, count_ref, seg_ref, samples_ref, table_ref, out_ref, pos_s, g_s):
    tiles = STEP // 32
    sample = lax.broadcasted_iota(jnp.int32, (CELLS, STEP), 0)
    live = sample < count_ref[...]
    pos = jnp.where(live, pos_ref[...].astype(jnp.float32) * 0.4, -100.0)
    pos_s[:, 0:CELLS] = pos.T
    mids = (lax.broadcasted_iota(jnp.int32, (CELLS, 256), 0).astype(jnp.float32) + 0.5) * 0.4
    low = lax.broadcasted_iota(jnp.int32, (8, 128), 1) < 64
    sub = lax.broadcasted_iota(jnp.int32, (32, 128), 0) % 8
    lane_half = lax.broadcasted_iota(jnp.int32, (32, 128), 1) // 64
    keep = lane_half == sub % 2
    group = sub // 2

    def one_tile(t, carry):
        start = pl.multiple_of(t * 32, 32)
        pos_rows = pos_s[pl.ds(start, 32), :]
        halves = []
        for h in range(2):
            even = pos_rows[16 * h : 16 * h + 8]
            odd = pltpu.roll(pos_rows[16 * h + 8 : 16 * h + 16], 64, 1)
            halves.append(jnp.where(low, even, odd))
        row4 = jnp.concatenate(halves, axis=1)
        parts = []
        for nb in range(8):
            offset = row4[nb : nb + 1, :] - mids
            bump = jnp.maximum(1.0 - offset * offset, 0.0)
            parts.append((bump * bump).astype(jnp.bfloat16))
        weights = jnp.concatenate(parts, axis=0)
        vals = samples_ref[pl.ds(start, 32), :].astype(jnp.float32)
        zero = jnp.zeros((8, 128), jnp.float32)
        lhs = []
        for p in range(2):
            for kb in range(4):
                piece = vals[8 * kb : 8 * kb + 8]
                if kb % 2 != p:
                    piece = pltpu.roll(piece, 64, 1)
                piece = jnp.where(low == (kb % 2 == 0), piece, 0.0)
                lhs.append(jnp.concatenate([piece, zero] if kb < 2 else [zero, piece], axis=1))
        lhs = jnp.concatenate(lhs, axis=0).astype(jnp.bfloat16)
        full = lax.dot_general(lhs, weights, NT, preferred_element_type=jnp.float32)
        sides = []
        for p in range(2):
            block = full[32 * p : 32 * p + 32]
            own = jnp.where(group == 0, block[:, 0:128], block[:, 128:256])
            own = jnp.where(group == 2, block[:, 256:384], own)
            own = jnp.where(group == 3, block[:, 384:512], own)
            sides.append(jnp.where(keep, own, 0.0))
        g_s[pl.ds(start, 32), :] = jnp.concatenate(sides, axis=1).astype(jnp.bfloat16)
        return carry

    lax.fori_loop(0, tiles, one_tile, 0, unroll=2)
    every = lax.dot_general(table_ref[...], g_s[...], NT, preferred_element_type=jnp.float32)
    seg = seg_ref[...]
    own = jnp.where(seg == 0, every[0:32], every[32:64])
    own = jnp.where(seg == 2, every[64:96], own)
    own = jnp.where(seg == 3, every[96:128], own)
    out_ref[...] = own.astype(jnp.bfloat16)


def grid_blocks(pos_t, count, seg, samples, table):
    blocks = samples.shape[0]
    return pl.pallas_call(
        grid_kernel,
        grid=(blocks // STEP,),
        in_specs=[
            pl.BlockSpec((CELLS, STEP), lambda i: (0, i)),
            pl.BlockSpec((1, STEP), lambda i: (0, i)),
            pl.BlockSpec((1, STEP), lambda i: (0, i)),
            pl.BlockSpec((STEP, 128), lambda i: (i, 0)),
            pl.BlockSpec((128, 256), lambda i: (0, 0)),
        ],
        out_specs=pl.BlockSpec((32, STEP), lambda i: (0, i)),
        out_shape=jax.ShapeDtypeStruct((32, blocks), jnp.bfloat16),
        scratch_shapes=[pltpu.VMEM((STEP, 128), jnp.float32), pltpu.VMEM((STEP, 256), jnp.bfloat16)],
        compiler_params=pltpu.CompilerParams(vmem_limit_bytes=48 * 1024 * 1024),
        name="grid_blocks",
    )(pos_t, count, seg, samples, table)


def place_kernel(values_ref, index_ref, y_ref, z_ref, out_ref, acc):
    first = (pl.program_id(0) == 0) & (pl.program_id(1) == 0)
    last = (pl.program_id(0) == pl.num_programs(0) - 1) & (pl.program_id(1) == pl.num_programs(1) - 1)

    @pl.when(first)
    def _():
        acc[...] = jnp.zeros_like(acc)

    iota = lax.broadcasted_iota(jnp.int32, (256, GATHER), 0).astype(jnp.float32).astype(jnp.bfloat16)
    depth = index_ref[0, 0:1, :]
    line = index_ref[0, 1:2, :]
    one = jnp.ones((), jnp.bfloat16)
    zero = jnp.zeros((), jnp.bfloat16)
    planes = jnp.where(iota == depth, one, zero)
    hit = iota == line
    for p in range(2):
        spread = jnp.where(hit, values_ref[0, p : p + 1, :], zero)
        acc[256 * p : 256 * p + 256, :] += lax.dot_general(
            spread, planes, NT, preferred_element_type=jnp.float32
        )

    @pl.when(last)
    def _():
        x_rows = acc[...].astype(jnp.bfloat16)
        y_t = jnp.dot(y_ref[...], x_rows, preferred_element_type=jnp.float32).astype(jnp.bfloat16)
        real, imag = y_t[0:256], y_t[256:512]

        def turn(table, side):
            return lax.dot_general(table, side, NT, preferred_element_type=jnp.float32)

        out_ref[:, 0:256] = (turn(z_ref[0], real) + turn(z_ref[2], imag)).astype(jnp.bfloat16)
        out_ref[:, 256:512] = (turn(z_ref[1], real) + turn(z_ref[0], imag)).astype(jnp.bfloat16)


def place_blocks(values, index, y_table, z_tables):
    sources, _, blocks = values.shape
    return pl.pallas_call(
        place_kernel,
        grid=(sources, blocks // GATHER),
        in_specs=[
            pl.BlockSpec((1, 2, GATHER), lambda i, j: (i, 0, j)),
            pl.BlockSpec((1, 2, GATHER), lambda i, j: (i, 0, j)),
            pl.BlockSpec((512, 512), lambda i, j: (0, 0)),
            pl.BlockSpec((3, 256, 256), lambda i, j: (0, 0, 0)),
        ],
        out_specs=pl.BlockSpec((256, 512), lambda i, j: (0, 0)),
        out_shape=jax.ShapeDtypeStruct((256, 512), jnp.bfloat16),
        scratch_shapes=[pltpu.VMEM((512, 256), jnp.float32)],
        compiler_params=pltpu.CompilerParams(vmem_limit_bytes=48 * 1024 * 1024),
        name="place_blocks",
    )(values, index, y_table, z_tables)


def per_device(samples, sample_pos, block_count, grid_block, block_slab, sensitivity):
    slabs = lax.axis_size("slab")
    groups = lax.axis_size("coil")
    blocks = samples.shape[1]
    planes = sensitivity.shape[1]
    coils = sensitivity.shape[0]
    width = sensitivity.shape[2]
    row = block_slab[:, 0] * (planes * KY * 4) + grid_block
    index = jnp.stack([row // (KY * 4), row // 4 % KY]).astype(jnp.bfloat16)
    index = lax.all_gather(index, "slab", axis=0)
    moved = grid_blocks(
        sample_pos.T,
        block_count[None],
        (grid_block % 4)[None],
        samples[0],
        jnp.asarray(across_table(), jnp.bfloat16),
    )
    moved = moved.reshape(groups, 2 * width, blocks)
    moved = lax.all_to_all(moved, "coil", split_axis=0, concat_axis=0, tiled=True)
    moved = moved.reshape(slabs, 2, blocks)
    moved = lax.all_to_all(moved, "slab", split_axis=0, concat_axis=0, tiled=True)
    whole = place_blocks(
        moved,
        index,
        jnp.asarray(line_table(KY), jnp.bfloat16),
        jnp.asarray(depth_tables(Z), jnp.bfloat16),
    )
    whole = whole.reshape(slabs, planes, 2 * KY)
    own = lax.all_to_all(whole, "slab", split_axis=0, concat_axis=0, tiled=True)
    own = jnp.swapaxes(own.reshape(coils, width, planes, 2 * KY), 1, 2).astype(jnp.float32)
    maps = sensitivity.astype(jnp.float32)
    map_re, map_im = maps[..., :KY], maps[..., KY:]
    img_re, img_im = own[..., :KY], own[..., KY:]
    real_part = jnp.sum(map_re * img_re + map_im * img_im, axis=0)
    imag_part = jnp.sum(map_re * img_im - map_im * img_re, axis=0)
    return jnp.concatenate([real_part, imag_part], axis=-1)


def solution(mesh):
    return jax.shard_map(
        per_device,
        mesh=mesh,
        in_specs=(
            P("coil", "slab", None),
            P("slab", None),
            P("slab"),
            P("slab"),
            P("slab", None),
            P(None, "slab", "coil", None),
        ),
        out_specs=P("slab", "coil", None),
        check_vma=False,
    )
```

```python
import functools
import math

import jax
import jax.numpy as jnp
import numpy as np
from jax import lax
from jax.experimental import pallas as pl
from jax.experimental.pallas import tpu as pltpu
from jax.sharding import PartitionSpec as P

KX = 256
KY = 256
Z = 256
XW = 16
CELLS = 64
STEP = 1024
GATHER = 8192
NT = (((1,), (1,)), ((), ()))


def twiddle(first, second, length):
    phase = (first * second % length).astype(np.float32) * np.float32(2.0 * math.pi / length)
    scale = 1.0 / math.sqrt(length)
    return np.cos(phase) * scale, np.sin(phase) * scale


def across_table():
    cell = np.arange(CELLS)
    rows = (KX - XW) // 2 + np.arange(XW)
    table = np.zeros((KX // CELLS, XW, 2, 2, 2, CELLS), np.float32)
    for s in range(KX // CELLS):
        cosine, sine = twiddle((s * CELLS + cell)[None, :], rows[:, None], KX)
        table[s, :, 0, 0] = cosine[:, None, :]
        table[s, :, 1, 0] = sine[:, None, :]
        table[s, :, 0, 1] = -sine[:, None, :]
        table[s, :, 1, 1] = cosine[:, None, :]
    return table.reshape(KX // CELLS * XW * 2, 4 * CELLS)


def line_table(length):
    index = np.arange(length)
    cosine, sine = twiddle(index[:, None], index[None, :], length)
    return np.block([[cosine, -sine], [sine, cosine]])


def depth_tables(length):
    index = np.arange(length)
    cosine, sine = twiddle(index[:, None], index[None, :], length)
    return np.stack([cosine, sine, -sine])


def grid_kernel(pos_ref, count_ref, seg_ref, samples_ref, table_ref, out_ref, pos_s, g_s):
    tiles = STEP // 32
    sample = lax.broadcasted_iota(jnp.int32, (CELLS, STEP), 0)
    live = sample < count_ref[...]
    pos = jnp.where(live, pos_ref[...].astype(jnp.float32) * 0.4, -100.0)
    pos_s[:, 0:CELLS] = pos.T
    mids = (lax.broadcasted_iota(jnp.int32, (CELLS, 256), 0).astype(jnp.float32) + 0.5) * 0.4
    low = lax.broadcasted_iota(jnp.int32, (8, 128), 1) < 64
    sub = lax.broadcasted_iota(jnp.int32, (32, 128), 0) % 8
    lane_half = lax.broadcasted_iota(jnp.int32, (32, 128), 1) // 64
    keep = lane_half == sub % 2
    group = sub // 2

    def one_tile(t, carry):
        start = pl.multiple_of(t * 32, 32)
        pos_rows = pos_s[pl.ds(start, 32), :]
        halves = []
        for h in range(2):
            even = pos_rows[16 * h : 16 * h + 8]
            odd = pltpu.roll(pos_rows[16 * h + 8 : 16 * h + 16], 64, 1)
            halves.append(jnp.where(low, even, odd))
        row4 = jnp.concatenate(halves, axis=1)
        parts = []
        for nb in range(8):
            offset = row4[nb : nb + 1, :] - mids
            bump = jnp.maximum(1.0 - offset * offset, 0.0)
            parts.append((bump * bump).astype(jnp.bfloat16))
        weights = jnp.concatenate(parts, axis=0)
        vals = samples_ref[pl.ds(start, 32), :].astype(jnp.float32)
        zero = jnp.zeros((8, 128), jnp.float32)
        lhs = []
        for p in range(2):
            for kb in range(4):
                piece = vals[8 * kb : 8 * kb + 8]
                if kb % 2 != p:
                    piece = pltpu.roll(piece, 64, 1)
                piece = jnp.where(low == (kb % 2 == 0), piece, 0.0)
                lhs.append(jnp.concatenate([piece, zero] if kb < 2 else [zero, piece], axis=1))
        lhs = jnp.concatenate(lhs, axis=0).astype(jnp.bfloat16)
        full = lax.dot_general(lhs, weights, NT, preferred_element_type=jnp.float32)
        sides = []
        for p in range(2):
            block = full[32 * p : 32 * p + 32]
            own = jnp.where(group == 0, block[:, 0:128], block[:, 128:256])
            own = jnp.where(group == 2, block[:, 256:384], own)
            own = jnp.where(group == 3, block[:, 384:512], own)
            sides.append(jnp.where(keep, own, 0.0))
        g_s[pl.ds(start, 32), :] = jnp.concatenate(sides, axis=1).astype(jnp.bfloat16)
        return carry

    lax.fori_loop(0, tiles, one_tile, 0, unroll=True)
    every = lax.dot_general(table_ref[...], g_s[...], NT, preferred_element_type=jnp.float32)
    seg = seg_ref[...]
    own = jnp.where(seg == 0, every[0:32], every[32:64])
    own = jnp.where(seg == 2, every[64:96], own)
    own = jnp.where(seg == 3, every[96:128], own)
    out_ref[...] = own.astype(jnp.bfloat16)


def grid_blocks(pos_t, count, seg, samples, table):
    blocks = samples.shape[0]
    return pl.pallas_call(
        grid_kernel,
        grid=(blocks // STEP,),
        in_specs=[
            pl.BlockSpec((CELLS, STEP), lambda i: (0, i)),
            pl.BlockSpec((1, STEP), lambda i: (0, i)),
            pl.BlockSpec((1, STEP), lambda i: (0, i)),
            pl.BlockSpec((STEP, 128), lambda i: (i, 0)),
            pl.BlockSpec((128, 256), lambda i: (0, 0)),
        ],
        out_specs=pl.BlockSpec((32, STEP), lambda i: (0, i)),
        out_shape=jax.ShapeDtypeStruct((32, blocks), jnp.bfloat16),
        scratch_shapes=[pltpu.VMEM((STEP, 128), jnp.float32), pltpu.VMEM((STEP, 256), jnp.bfloat16)],
        compiler_params=pltpu.CompilerParams(vmem_limit_bytes=48 * 1024 * 1024),
        name="grid_blocks",
    )(pos_t, count, seg, samples, table)


def place_kernel(values_ref, index_ref, y_ref, z_ref, out_ref, acc):
    first = (pl.program_id(0) == 0) & (pl.program_id(1) == 0)
    last = (pl.program_id(0) == pl.num_programs(0) - 1) & (pl.program_id(1) == pl.num_programs(1) - 1)

    @pl.when(first)
    def _():
        acc[...] = jnp.zeros_like(acc)

    iota = lax.broadcasted_iota(jnp.int32, (256, GATHER), 0).astype(jnp.float32).astype(jnp.bfloat16)
    index = index_ref[0].astype(jnp.float32).astype(jnp.bfloat16)
    one = jnp.ones((), jnp.bfloat16)
    zero = jnp.zeros((), jnp.bfloat16)
    planes = jnp.where(iota == index[0:1], one, zero)
    hit = iota == index[1:2]
    spread = [jnp.where(hit, values_ref[0, p : p + 1, :], zero) for p in range(2)]
    acc[...] += lax.dot_general(
        jnp.concatenate(spread, axis=0), planes, NT, preferred_element_type=jnp.float32
    )

    @pl.when(last)
    def _():
        x_rows = acc[...].astype(jnp.bfloat16)
        y_t = jnp.dot(y_ref[...], x_rows, preferred_element_type=jnp.float32).astype(jnp.bfloat16)
        real, imag = y_t[0:256], y_t[256:512]

        def turn(table, side):
            return lax.dot_general(table, side, NT, preferred_element_type=jnp.float32)

        out_ref[:, 0:256] = (turn(z_ref[0], real) + turn(z_ref[2], imag)).astype(jnp.bfloat16)
        out_ref[:, 256:512] = (turn(z_ref[1], real) + turn(z_ref[0], imag)).astype(jnp.bfloat16)


def place_blocks(values, index, y_table, z_tables):
    sources, _, blocks = values.shape
    return pl.pallas_call(
        place_kernel,
        grid=(sources, blocks // GATHER),
        in_specs=[
            pl.BlockSpec((1, 2, GATHER), lambda i, j: (i, 0, j)),
            pl.BlockSpec((1, 2, GATHER), lambda i, j: (i, 0, j)),
            pl.BlockSpec((512, 512), lambda i, j: (0, 0)),
            pl.BlockSpec((3, 256, 256), lambda i, j: (0, 0, 0)),
        ],
        out_specs=pl.BlockSpec((256, 512), lambda i, j: (0, 0)),
        out_shape=jax.ShapeDtypeStruct((256, 512), jnp.bfloat16),
        scratch_shapes=[pltpu.VMEM((512, 256), jnp.float32)],
        compiler_params=pltpu.CompilerParams(vmem_limit_bytes=48 * 1024 * 1024),
        name="place_blocks",
    )(values, index, y_table, z_tables)


def per_device(samples, sample_pos, block_count, grid_block, block_slab, sensitivity):
    slabs = lax.axis_size("slab")
    groups = lax.axis_size("coil")
    blocks = samples.shape[1]
    planes = sensitivity.shape[1]
    coils = sensitivity.shape[0]
    width = sensitivity.shape[2]
    row = block_slab[:, 0] * (planes * KY * 4) + grid_block
    index = jnp.stack([row // (KY * 4), row // 4 % KY])
    index = lax.all_gather(index, "slab", axis=0)
    moved = grid_blocks(
        sample_pos.T,
        block_count[None],
        (grid_block % 4)[None],
        samples[0],
        jnp.asarray(across_table(), jnp.bfloat16),
    )
    moved = moved.reshape(groups, 2 * width, blocks)
    moved = lax.all_to_all(moved, "coil", split_axis=0, concat_axis=0, tiled=True)
    moved = moved.reshape(slabs, 2, blocks)
    moved = lax.all_to_all(moved, "slab", split_axis=0, concat_axis=0, tiled=True)
    whole = place_blocks(
        moved,
        index,
        jnp.asarray(line_table(KY), jnp.bfloat16),
        jnp.asarray(depth_tables(Z), jnp.bfloat16),
    )
    whole = whole.reshape(slabs, planes, 2 * KY)
    own = lax.all_to_all(whole, "slab", split_axis=0, concat_axis=0, tiled=True)
    own = jnp.swapaxes(own.reshape(coils, width, planes, 2 * KY), 1, 2).astype(jnp.float32)
    maps = sensitivity.astype(jnp.float32)
    map_re, map_im = maps[..., :KY], maps[..., KY:]
    img_re, img_im = own[..., :KY], own[..., KY:]
    real_part = jnp.sum(map_re * img_re + map_im * img_im, axis=0)
    imag_part = jnp.sum(map_re * img_im - map_im * img_re, axis=0)
    return jnp.concatenate([real_part, imag_part], axis=-1)


def solution(mesh):
    return jax.shard_map(
        per_device,
        mesh=mesh,
        in_specs=(
            P("coil", "slab", None),
            P("slab", None),
            P("slab"),
            P("slab"),
            P("slab", None),
            P(None, "slab", "coil", None),
        ),
        out_specs=P("slab", "coil", None),
        check_vma=False,
    )
```

```python
import functools
import math

import jax
import jax.numpy as jnp
import numpy as np
from jax import lax
from jax.experimental import pallas as pl
from jax.experimental.pallas import tpu as pltpu
from jax.sharding import PartitionSpec as P

KX = 256
KY = 256
Z = 256
XW = 16
CELLS = 64
SLABS = 16
STEP = 1024
TOGETHER = 4
NT = (((1,), (1,)), ((), ()))


def twiddle(first, second, length):
    phase = (first * second % length).astype(np.float32) * np.float32(2.0 * math.pi / length)
    scale = 1.0 / math.sqrt(length)
    return np.cos(phase) * scale, np.sin(phase) * scale


def across_table():
    cell = np.arange(CELLS)
    rows = (KX - XW) // 2 + np.arange(XW)
    table = np.zeros((KX // CELLS, XW, 2, 2, 2, CELLS), np.float32)
    for s in range(KX // CELLS):
        cosine, sine = twiddle((s * CELLS + cell)[None, :], rows[:, None], KX)
        table[s, :, 0, 0] = cosine[:, None, :]
        table[s, :, 1, 0] = sine[:, None, :]
        table[s, :, 0, 1] = -sine[:, None, :]
        table[s, :, 1, 1] = cosine[:, None, :]
    return table.reshape(KX // CELLS * XW * 2, 4 * CELLS)


def line_table(length):
    index = np.arange(length)
    cosine, sine = twiddle(index[:, None], index[None, :], length)
    return np.block([[cosine, -sine], [sine, cosine]])


def depth_tables(length):
    index = np.arange(length)
    cosine, sine = twiddle(index[:, None], index[None, :], length)
    return np.stack([cosine, sine, -sine])


def grid_kernel(pos_ref, count_ref, row_ref, slab_ref, samples_ref, table_ref, out_ref, index_ref, pos_s, g_s):
    tiles = STEP // 32
    sample = lax.broadcasted_iota(jnp.int32, (CELLS, STEP), 0)
    live = sample < count_ref[...]
    pos = jnp.where(live, pos_ref[...].astype(jnp.float32) * 0.4, -100.0)
    pos_s[:, 0:CELLS] = pos.T
    mids = (lax.broadcasted_iota(jnp.int32, (CELLS, 256), 0).astype(jnp.float32) + 0.5) * 0.4
    low = lax.broadcasted_iota(jnp.int32, (8, 128), 1) < 64
    sub = lax.broadcasted_iota(jnp.int32, (32, 128), 0) % 8
    lane_half = lax.broadcasted_iota(jnp.int32, (32, 128), 1) // 64
    keep = lane_half == sub % 2
    group = sub // 2

    def one_tile(t, carry):
        start = pl.multiple_of(t * 32, 32)
        pos_rows = pos_s[pl.ds(start, 32), :]
        halves = []
        for h in range(2):
            even = pos_rows[16 * h : 16 * h + 8]
            odd = pltpu.roll(pos_rows[16 * h + 8 : 16 * h + 16], 64, 1)
            halves.append(jnp.where(low, even, odd))
        row4 = jnp.concatenate(halves, axis=1)
        parts = []
        for nb in range(8):
            offset = row4[nb : nb + 1, :] - mids
            bump = jnp.maximum(1.0 - offset * offset, 0.0)
            parts.append((bump * bump).astype(jnp.bfloat16))
        weights = jnp.concatenate(parts, axis=0)
        vals = samples_ref[pl.ds(start, 32), :].astype(jnp.float32)
        zero = jnp.zeros((8, 128), jnp.float32)
        lhs = []
        for p in range(2):
            for kb in range(4):
                piece = vals[8 * kb : 8 * kb + 8]
                if kb % 2 != p:
                    piece = pltpu.roll(piece, 64, 1)
                piece = jnp.where(low == (kb % 2 == 0), piece, 0.0)
                lhs.append(jnp.concatenate([piece, zero] if kb < 2 else [zero, piece], axis=1))
        lhs = jnp.concatenate(lhs, axis=0).astype(jnp.bfloat16)
        full = lax.dot_general(lhs, weights, NT, preferred_element_type=jnp.float32)
        sides = []
        for p in range(2):
            block = full[32 * p : 32 * p + 32]
            own = jnp.where(group == 0, block[:, 0:128], block[:, 128:256])
            own = jnp.where(group == 2, block[:, 256:384], own)
            own = jnp.where(group == 3, block[:, 384:512], own)
            sides.append(jnp.where(keep, own, 0.0))
        g_s[pl.ds(start, 32), :] = jnp.concatenate(sides, axis=1).astype(jnp.bfloat16)
        return carry

    lax.fori_loop(0, tiles, one_tile, 0, unroll=True)
    every = lax.dot_general(table_ref[...], g_s[...], NT, preferred_element_type=jnp.float32)
    row = row_ref[...]
    seg = row % 4
    plane_rows = KY * KX // CELLS
    depth = slab_ref[...] * (Z // SLABS) + row // plane_rows
    line = row // (KX // CELLS) % KY
    index_ref[...] = jnp.concatenate([depth, line], axis=0).astype(jnp.float32).astype(jnp.bfloat16)
    own = jnp.where(seg == 0, every[0:32], every[32:64])
    own = jnp.where(seg == 2, every[64:96], own)
    own = jnp.where(seg == 3, every[96:128], own)
    out_ref[...] = own.astype(jnp.bfloat16)


def grid_blocks(pos_t, count, row, slab, samples, table, first, blocks):
    skip = first // STEP
    return pl.pallas_call(
        grid_kernel,
        grid=(blocks // STEP,),
        in_specs=[
            pl.BlockSpec((CELLS, STEP), lambda i: (0, i + skip)),
            pl.BlockSpec((1, STEP), lambda i: (0, i + skip)),
            pl.BlockSpec((1, STEP), lambda i: (0, i + skip)),
            pl.BlockSpec((1, STEP), lambda i: (0, i + skip)),
            pl.BlockSpec((STEP, 128), lambda i: (i + skip, 0)),
            pl.BlockSpec((128, 256), lambda i: (0, 0)),
        ],
        out_specs=[
            pl.BlockSpec((2 * XW, STEP), lambda i: (0, i)),
            pl.BlockSpec((2, STEP), lambda i: (0, i)),
        ],
        out_shape=[
            jax.ShapeDtypeStruct((2 * XW, blocks), jnp.bfloat16),
            jax.ShapeDtypeStruct((2, blocks), jnp.bfloat16),
        ],
        scratch_shapes=[pltpu.VMEM((STEP, 128), jnp.float32), pltpu.VMEM((STEP, 256), jnp.bfloat16)],
        compiler_params=pltpu.CompilerParams(vmem_limit_bytes=60 * 1024 * 1024),
        cost_estimate=pl.CostEstimate(
            flops=4 * blocks * CELLS * 16 * CELLS, bytes_accessed=8 * blocks * CELLS, transcendentals=0
        ),
        name="grid_blocks",
    )(pos_t, count, row, slab, samples, table)


def place_step(values_ref, acc):
    sources, _, length = values_ref.shape
    iota = lax.broadcasted_iota(jnp.int32, (256, length), 0).astype(jnp.float32).astype(jnp.bfloat16)
    one = jnp.ones((), jnp.bfloat16)
    zero = jnp.zeros((), jnp.bfloat16)
    planes, spread = [], []
    for i in range(sources):
        rows = values_ref[i]
        planes.append(jnp.where(iota == rows[2:3], one, zero))
        hit = iota == rows[3:4]
        both = [jnp.where(hit, rows[p : p + 1], zero) for p in range(2)]
        spread.append(jnp.concatenate(both, axis=0))
    acc[...] += lax.dot_general(
        jnp.concatenate(spread, axis=1),
        jnp.concatenate(planes, axis=1),
        NT,
        preferred_element_type=jnp.float32,
    )


def place_first_kernel(values_ref, acc_ref):
    @pl.when(pl.program_id(0) == 0)
    def _():
        acc_ref[...] = jnp.zeros_like(acc_ref)

    place_step(values_ref, acc_ref)


def place_last_kernel(values_ref, start_ref, y_ref, z_ref, out_ref, acc):
    @pl.when(pl.program_id(0) == 0)
    def _():
        acc[...] = start_ref[...]

    place_step(values_ref, acc)

    @pl.when(pl.program_id(0) == pl.num_programs(0) - 1)
    def _():
        x_rows = acc[...].astype(jnp.bfloat16)
        y_t = jnp.dot(y_ref[...], x_rows, preferred_element_type=jnp.float32).astype(jnp.bfloat16)
        real, imag = y_t[0:256], y_t[256:512]

        def turn(table, side):
            return lax.dot_general(table, side, NT, preferred_element_type=jnp.float32)

        out_ref[:, 0:256] = (turn(z_ref[0], real) + turn(z_ref[2], imag)).astype(jnp.bfloat16)
        out_ref[:, 256:512] = (turn(z_ref[1], real) + turn(z_ref[0], imag)).astype(jnp.bfloat16)


def place_cost(values):
    sources, _, blocks = values.shape
    return pl.CostEstimate(
        flops=4 * sources * blocks * KY * Z, bytes_accessed=8 * sources * blocks, transcendentals=0
    )


def place_first(values):
    sources, rows, blocks = values.shape
    return pl.pallas_call(
        place_first_kernel,
        grid=(sources // TOGETHER,),
        in_specs=[pl.BlockSpec((TOGETHER, rows, blocks), lambda i: (i, 0, 0))],
        out_specs=pl.BlockSpec((2 * KY, Z), lambda i: (0, 0)),
        out_shape=jax.ShapeDtypeStruct((2 * KY, Z), jnp.float32),
        compiler_params=pltpu.CompilerParams(vmem_limit_bytes=44 * 1024 * 1024),
        cost_estimate=place_cost(values),
        name="place_first",
    )(values)


def place_last(values, start, y_table, z_tables):
    sources, rows, blocks = values.shape
    return pl.pallas_call(
        place_last_kernel,
        grid=(sources // TOGETHER,),
        in_specs=[
            pl.BlockSpec((TOGETHER, rows, blocks), lambda i: (i, 0, 0)),
            pl.BlockSpec((2 * KY, Z), lambda i: (0, 0)),
            pl.BlockSpec((2 * KY, 2 * KY), lambda i: (0, 0)),
            pl.BlockSpec((3, Z, Z), lambda i: (0, 0, 0)),
        ],
        out_specs=pl.BlockSpec((Z, 2 * KY), lambda i: (0, 0)),
        out_shape=jax.ShapeDtypeStruct((Z, 2 * KY), jnp.bfloat16),
        scratch_shapes=[pltpu.VMEM((2 * KY, Z), jnp.float32)],
        compiler_params=pltpu.CompilerParams(vmem_limit_bytes=44 * 1024 * 1024),
        cost_estimate=place_cost(values),
        name="place_last",
    )(values, start, y_table, z_tables)


def per_device(samples, sample_pos, block_count, grid_block, block_slab, sensitivity):
    slabs = lax.axis_size("slab")
    groups = lax.axis_size("coil")
    blocks = samples.shape[1]
    planes = sensitivity.shape[1]
    coils = sensitivity.shape[0]
    width = sensitivity.shape[2]
    table = jnp.asarray(across_table(), jnp.bfloat16)
    half = blocks // 2
    sent = []
    for part in range(2):
        moved, index = grid_blocks(
            sample_pos.T,
            block_count[None],
            grid_block[None],
            block_slab.reshape(1, blocks),
            samples[0],
            table,
            part * half,
            half,
        )
        index = jnp.broadcast_to(index[None], (slabs, 2, half))
        sent.append(jnp.concatenate([moved.reshape(slabs, 2, half), index], axis=1))
    early = lax.all_to_all(sent[0], "slab", split_axis=0, concat_axis=0, tiled=True)
    early, later = lax.optimization_barrier((early, sent[1]))
    later = lax.all_to_all(later, "slab", split_axis=0, concat_axis=0, tiled=True)
    whole = place_last(
        later,
        place_first(early),
        jnp.asarray(line_table(KY), jnp.bfloat16),
        jnp.asarray(depth_tables(Z), jnp.bfloat16),
    )
    whole = whole.reshape(slabs, planes, 2 * KY)
    own = lax.all_to_all(whole, "slab", split_axis=0, concat_axis=0, tiled=True)
    own = own.reshape(groups, width, planes, 2 * KY)
    own = lax.all_to_all(own, "coil", split_axis=0, concat_axis=0, tiled=True)
    own = jnp.swapaxes(own.reshape(coils, width, planes, 2 * KY), 1, 2).astype(jnp.float32)
    maps = sensitivity.astype(jnp.float32)
    map_re, map_im = maps[..., :KY], maps[..., KY:]
    img_re, img_im = own[..., :KY], own[..., KY:]
    real_part = jnp.sum(map_re * img_re + map_im * img_im, axis=0)
    imag_part = jnp.sum(map_re * img_im - map_im * img_re, axis=0)
    return jnp.concatenate([real_part, imag_part], axis=-1)


def solution(mesh):
    return jax.shard_map(
        per_device,
        mesh=mesh,
        in_specs=(
            P("coil", "slab", None),
            P("slab", None),
            P("slab"),
            P("slab"),
            P("slab", None),
            P(None, "slab", "coil", None),
        ),
        out_specs=P("slab", "coil", None),
        check_vma=False,
    )
```

```python
import functools
import math

import jax
import jax.numpy as jnp
import numpy as np
from jax import lax
from jax.experimental import pallas as pl
from jax.experimental.pallas import tpu as pltpu
from jax.sharding import PartitionSpec as P

KX = 256
KY = 256
Z = 256
XW = 16
CELLS = 64
SLABS = 16
STEP = 1024
TOGETHER = 4
NT = (((1,), (1,)), ((), ()))


def twiddle(first, second, length):
    phase = (first * second % length).astype(np.float32) * np.float32(2.0 * math.pi / length)
    scale = 1.0 / math.sqrt(length)
    return np.cos(phase) * scale, np.sin(phase) * scale


def across_table():
    cell = np.arange(CELLS)
    rows = (KX - XW) // 2 + np.arange(XW)
    table = np.zeros((KX // CELLS, XW, 2, 2, 2, CELLS), np.float32)
    for s in range(KX // CELLS):
        cosine, sine = twiddle((s * CELLS + cell)[None, :], rows[:, None], KX)
        table[s, :, 0, 0] = cosine[:, None, :]
        table[s, :, 1, 0] = sine[:, None, :]
        table[s, :, 0, 1] = -sine[:, None, :]
        table[s, :, 1, 1] = cosine[:, None, :]
    return table.reshape(KX // CELLS * XW * 2, 4 * CELLS)


def line_table(length):
    index = np.arange(length)
    cosine, sine = twiddle(index[:, None], index[None, :], length)
    return np.block([[cosine, -sine], [sine, cosine]])


def depth_tables(length):
    index = np.arange(length)
    cosine, sine = twiddle(index[:, None], index[None, :], length)
    return np.stack([cosine, sine, -sine])


def grid_kernel(pos_ref, count_ref, row_ref, slab_ref, samples_ref, table_ref, out_ref, pos_s, g_s):
    tiles = STEP // 32
    sample = lax.broadcasted_iota(jnp.int32, (CELLS, STEP), 0)
    live = sample < count_ref[...]
    pos = jnp.where(live, pos_ref[...].astype(jnp.float32) * 0.4, -100.0)
    pos_s[:, 0:CELLS] = pos.T
    mids = (lax.broadcasted_iota(jnp.int32, (CELLS, 256), 0).astype(jnp.float32) + 0.5) * 0.4
    low = lax.broadcasted_iota(jnp.int32, (8, 128), 1) < 64
    sub = lax.broadcasted_iota(jnp.int32, (32, 128), 0) % 8
    lane_half = lax.broadcasted_iota(jnp.int32, (32, 128), 1) // 64
    keep = lane_half == sub % 2
    group = sub // 2

    def one_tile(t, carry):
        start = pl.multiple_of(t * 32, 32)
        pos_rows = pos_s[pl.ds(start, 32), :]
        halves = []
        for h in range(2):
            even = pos_rows[16 * h : 16 * h + 8]
            odd = pltpu.roll(pos_rows[16 * h + 8 : 16 * h + 16], 64, 1)
            halves.append(jnp.where(low, even, odd))
        row4 = jnp.concatenate(halves, axis=1)
        parts = []
        for nb in range(8):
            offset = row4[nb : nb + 1, :] - mids
            bump = jnp.maximum(1.0 - offset * offset, 0.0)
            parts.append((bump * bump).astype(jnp.bfloat16))
        weights = jnp.concatenate(parts, axis=0)
        vals = samples_ref[pl.ds(start, 32), :].astype(jnp.float32)
        zero = jnp.zeros((8, 128), jnp.float32)
        lhs = []
        for p in range(2):
            for kb in range(4):
                piece = vals[8 * kb : 8 * kb + 8]
                if kb % 2 != p:
                    piece = pltpu.roll(piece, 64, 1)
                piece = jnp.where(low == (kb % 2 == 0), piece, 0.0)
                lhs.append(jnp.concatenate([piece, zero] if kb < 2 else [zero, piece], axis=1))
        lhs = jnp.concatenate(lhs, axis=0).astype(jnp.bfloat16)
        full = lax.dot_general(lhs, weights, NT, preferred_element_type=jnp.float32)
        sides = []
        for p in range(2):
            block = full[32 * p : 32 * p + 32]
            own = jnp.where(group == 0, block[:, 0:128], block[:, 128:256])
            own = jnp.where(group == 2, block[:, 256:384], own)
            own = jnp.where(group == 3, block[:, 384:512], own)
            sides.append(jnp.where(keep, own, 0.0))
        g_s[pl.ds(start, 32), :] = jnp.concatenate(sides, axis=1).astype(jnp.bfloat16)
        return carry

    lax.fori_loop(0, tiles, one_tile, 0, unroll=True)
    every = lax.dot_general(table_ref[...], g_s[...], NT, preferred_element_type=jnp.float32)
    row = row_ref[...]
    seg = row % 4
    plane_rows = KY * KX // CELLS
    depth = slab_ref[...] * (Z // SLABS) + row // plane_rows
    line = row // (KX // CELLS) % KY
    index = jnp.concatenate([depth, line], axis=0).astype(jnp.float32)
    own = jnp.where(seg == 0, every[0:32], every[32:64])
    own = jnp.where(seg == 2, every[64:96], own)
    own = jnp.where(seg == 3, every[96:128], own)
    sent = jnp.concatenate(
        [own.reshape(XW, 2, STEP), jnp.broadcast_to(index[None], (XW, 2, STEP))], axis=1
    )
    out_ref[...] = sent.astype(jnp.bfloat16)


def grid_blocks(pos_t, count, row, slab, samples, table, first, blocks):
    skip = first // STEP
    return pl.pallas_call(
        grid_kernel,
        grid=(blocks // STEP,),
        in_specs=[
            pl.BlockSpec((CELLS, STEP), lambda i: (0, i + skip)),
            pl.BlockSpec((1, STEP), lambda i: (0, i + skip)),
            pl.BlockSpec((1, STEP), lambda i: (0, i + skip)),
            pl.BlockSpec((1, STEP), lambda i: (0, i + skip)),
            pl.BlockSpec((STEP, 128), lambda i: (i + skip, 0)),
            pl.BlockSpec((128, 256), lambda i: (0, 0)),
        ],
        out_specs=pl.BlockSpec((XW, 4, STEP), lambda i: (0, 0, i)),
        out_shape=jax.ShapeDtypeStruct((XW, 4, blocks), jnp.bfloat16),
        scratch_shapes=[pltpu.VMEM((STEP, 128), jnp.float32), pltpu.VMEM((STEP, 256), jnp.bfloat16)],
        compiler_params=pltpu.CompilerParams(vmem_limit_bytes=60 * 1024 * 1024),
        cost_estimate=pl.CostEstimate(
            flops=4 * blocks * CELLS * 16 * CELLS, bytes_accessed=8 * blocks * CELLS, transcendentals=0
        ),
        name="grid_blocks",
    )(pos_t, count, row, slab, samples, table)


def place_step(values_ref, acc):
    sources, _, length = values_ref.shape
    iota = lax.broadcasted_iota(jnp.int32, (256, length), 0).astype(jnp.float32).astype(jnp.bfloat16)
    one = jnp.ones((), jnp.bfloat16)
    zero = jnp.zeros((), jnp.bfloat16)
    planes, spread = [], []
    for i in range(sources):
        rows = values_ref[i]
        planes.append(jnp.where(iota == rows[2:3], one, zero))
        hit = iota == rows[3:4]
        both = [jnp.where(hit, rows[p : p + 1], zero) for p in range(2)]
        spread.append(jnp.concatenate(both, axis=0))
    acc[...] += lax.dot_general(
        jnp.concatenate(spread, axis=1),
        jnp.concatenate(planes, axis=1),
        NT,
        preferred_element_type=jnp.float32,
    )


def place_first_kernel(values_ref, acc_ref):
    @pl.when(pl.program_id(0) == 0)
    def _():
        acc_ref[...] = jnp.zeros_like(acc_ref)

    place_step(values_ref, acc_ref)


def place_last_kernel(values_ref, start_ref, y_ref, z_ref, out_ref, acc):
    @pl.when(pl.program_id(0) == 0)
    def _():
        acc[...] = start_ref[...]

    place_step(values_ref, acc)

    @pl.when(pl.program_id(0) == pl.num_programs(0) - 1)
    def _():
        x_rows = acc[...].astype(jnp.bfloat16)
        y_t = jnp.dot(y_ref[...], x_rows, preferred_element_type=jnp.float32).astype(jnp.bfloat16)
        real, imag = y_t[0:256], y_t[256:512]

        def turn(table, side):
            return lax.dot_general(table, side, NT, preferred_element_type=jnp.float32)

        out_ref[:, 0:256] = (turn(z_ref[0], real) + turn(z_ref[2], imag)).astype(jnp.bfloat16)
        out_ref[:, 256:512] = (turn(z_ref[1], real) + turn(z_ref[0], imag)).astype(jnp.bfloat16)


def place_cost(values):
    sources, _, blocks = values.shape
    return pl.CostEstimate(
        flops=4 * sources * blocks * KY * Z, bytes_accessed=8 * sources * blocks, transcendentals=0
    )


def place_first(values):
    sources, rows, blocks = values.shape
    return pl.pallas_call(
        place_first_kernel,
        grid=(sources // TOGETHER,),
        in_specs=[pl.BlockSpec((TOGETHER, rows, blocks), lambda i: (i, 0, 0))],
        out_specs=pl.BlockSpec((2 * KY, Z), lambda i: (0, 0)),
        out_shape=jax.ShapeDtypeStruct((2 * KY, Z), jnp.float32),
        compiler_params=pltpu.CompilerParams(vmem_limit_bytes=44 * 1024 * 1024),
        cost_estimate=place_cost(values),
        name="place_first",
    )(values)


def place_last(values, start, y_table, z_tables):
    sources, rows, blocks = values.shape
    return pl.pallas_call(
        place_last_kernel,
        grid=(sources // TOGETHER,),
        in_specs=[
            pl.BlockSpec((TOGETHER, rows, blocks), lambda i: (i, 0, 0)),
            pl.BlockSpec((2 * KY, Z), lambda i: (0, 0)),
            pl.BlockSpec((2 * KY, 2 * KY), lambda i: (0, 0)),
            pl.BlockSpec((3, Z, Z), lambda i: (0, 0, 0)),
        ],
        out_specs=pl.BlockSpec((Z, 2 * KY), lambda i: (0, 0)),
        out_shape=jax.ShapeDtypeStruct((Z, 2 * KY), jnp.bfloat16),
        scratch_shapes=[pltpu.VMEM((2 * KY, Z), jnp.float32)],
        compiler_params=pltpu.CompilerParams(vmem_limit_bytes=44 * 1024 * 1024),
        cost_estimate=place_cost(values),
        name="place_last",
    )(values, start, y_table, z_tables)


def per_device(samples, sample_pos, block_count, grid_block, block_slab, sensitivity):
    slabs = lax.axis_size("slab")
    groups = lax.axis_size("coil")
    blocks = samples.shape[1]
    planes = sensitivity.shape[1]
    coils = sensitivity.shape[0]
    width = sensitivity.shape[2]
    table = jnp.asarray(across_table(), jnp.bfloat16)
    half = blocks // 2
    sent = []
    for part in range(2):
        sent.append(
            grid_blocks(
                sample_pos.T,
                block_count[None],
                grid_block[None],
                block_slab.reshape(1, blocks),
                samples[0],
                table,
                part * half,
                half,
            )
        )
    early = lax.all_to_all(sent[0], "slab", split_axis=0, concat_axis=0, tiled=True)
    early, later = lax.optimization_barrier((early, sent[1]))
    later = lax.all_to_all(later, "slab", split_axis=0, concat_axis=0, tiled=True)
    whole = place_last(
        later,
        place_first(early),
        jnp.asarray(line_table(KY), jnp.bfloat16),
        jnp.asarray(depth_tables(Z), jnp.bfloat16),
    )
    whole = whole.reshape(slabs, planes, 2 * KY)
    own = lax.all_to_all(whole, "slab", split_axis=0, concat_axis=0, tiled=True)
    own = own.reshape(groups, width, planes, 2 * KY)
    own = lax.all_to_all(own, "coil", split_axis=0, concat_axis=0, tiled=True)
    own = jnp.swapaxes(own.reshape(coils, width, planes, 2 * KY), 1, 2).astype(jnp.float32)
    maps = sensitivity.astype(jnp.float32)
    map_re, map_im = maps[..., :KY], maps[..., KY:]
    img_re, img_im = own[..., :KY], own[..., KY:]
    real_part = jnp.sum(map_re * img_re + map_im * img_im, axis=0)
    imag_part = jnp.sum(map_re * img_im - map_im * img_re, axis=0)
    return jnp.concatenate([real_part, imag_part], axis=-1)


def solution(mesh):
    return jax.shard_map(
        per_device,
        mesh=mesh,
        in_specs=(
            P("coil", "slab", None),
            P("slab", None),
            P("slab"),
            P("slab"),
            P("slab", None),
            P(None, "slab", "coil", None),
        ),
        out_specs=P("slab", "coil", None),
        check_vma=False,
    )
```

```python
import functools
import math

import jax
import jax.numpy as jnp
import numpy as np
from jax import lax
from jax.experimental import pallas as pl
from jax.experimental.pallas import tpu as pltpu
from jax.sharding import PartitionSpec as P

KX = 256
KY = 256
Z = 256
XW = 16
CELLS = 64
SLABS = 16
STEP = 2048
TOGETHER = 8
NT = (((1,), (1,)), ((), ()))


def twiddle(first, second, length):
    phase = (first * second % length).astype(np.float32) * np.float32(2.0 * math.pi / length)
    scale = 1.0 / math.sqrt(length)
    return np.cos(phase) * scale, np.sin(phase) * scale


def across_table():
    cell = np.arange(CELLS)
    rows = (KX - XW) // 2 + np.arange(XW)
    table = np.zeros((KX // CELLS, XW, 2, 2, 2, CELLS), np.float32)
    for s in range(KX // CELLS):
        cosine, sine = twiddle((s * CELLS + cell)[None, :], rows[:, None], KX)
        table[s, :, 0, 0] = cosine[:, None, :]
        table[s, :, 1, 0] = sine[:, None, :]
        table[s, :, 0, 1] = -sine[:, None, :]
        table[s, :, 1, 1] = cosine[:, None, :]
    return table.reshape(KX // CELLS * XW * 2, 4 * CELLS)


def line_table(length):
    index = np.arange(length)
    cosine, sine = twiddle(index[:, None], index[None, :], length)
    return np.block([[cosine, -sine], [sine, cosine]])


def depth_tables(length):
    index = np.arange(length)
    cosine, sine = twiddle(index[:, None], index[None, :], length)
    return np.stack([cosine, sine, -sine])


def grid_kernel(pos_ref, count_ref, row_ref, slab_ref, samples_ref, table_ref, out_ref, pos_s, g_s):
    tiles = STEP // 32
    sample = lax.broadcasted_iota(jnp.int32, (CELLS, STEP), 0)
    live = sample < count_ref[...]
    pos = jnp.where(live, pos_ref[...].astype(jnp.float32) * 0.4, -100.0)
    pos_s[:, 0:CELLS] = pos.T
    mids = (lax.broadcasted_iota(jnp.int32, (CELLS, 256), 0).astype(jnp.float32) + 0.5) * 0.4
    low = lax.broadcasted_iota(jnp.int32, (8, 128), 1) < 64
    sub = lax.broadcasted_iota(jnp.int32, (32, 128), 0) % 8
    lane_half = lax.broadcasted_iota(jnp.int32, (32, 128), 1) // 64
    keep = lane_half == sub % 2
    group = sub // 2

    def one_tile(t, carry):
        start = pl.multiple_of(t * 32, 32)
        pos_rows = pos_s[pl.ds(start, 32), :]
        halves = []
        for h in range(2):
            even = pos_rows[16 * h : 16 * h + 8]
            odd = pltpu.roll(pos_rows[16 * h + 8 : 16 * h + 16], 64, 1)
            halves.append(jnp.where(low, even, odd))
        row4 = jnp.concatenate(halves, axis=1)
        parts = []
        for nb in range(8):
            offset = row4[nb : nb + 1, :] - mids
            bump = jnp.maximum(1.0 - offset * offset, 0.0)
            parts.append((bump * bump).astype(jnp.bfloat16))
        weights = jnp.concatenate(parts, axis=0)
        vals = samples_ref[pl.ds(start, 32), :].astype(jnp.float32)
        zero = jnp.zeros((8, 128), jnp.float32)
        lhs = []
        for p in range(2):
            for kb in range(4):
                piece = vals[8 * kb : 8 * kb + 8]
                if kb % 2 != p:
                    piece = pltpu.roll(piece, 64, 1)
                piece = jnp.where(low == (kb % 2 == 0), piece, 0.0)
                lhs.append(jnp.concatenate([piece, zero] if kb < 2 else [zero, piece], axis=1))
        lhs = jnp.concatenate(lhs, axis=0).astype(jnp.bfloat16)
        full = lax.dot_general(lhs, weights, NT, preferred_element_type=jnp.float32)
        sides = []
        for p in range(2):
            block = full[32 * p : 32 * p + 32]
            own = jnp.where(group == 0, block[:, 0:128], block[:, 128:256])
            own = jnp.where(group == 2, block[:, 256:384], own)
            own = jnp.where(group == 3, block[:, 384:512], own)
            sides.append(jnp.where(keep, own, 0.0))
        g_s[pl.ds(start, 32), :] = jnp.concatenate(sides, axis=1).astype(jnp.bfloat16)
        return carry

    lax.fori_loop(0, tiles, one_tile, 0, unroll=True)
    every = lax.dot_general(table_ref[...], g_s[...], NT, preferred_element_type=jnp.float32)
    row = row_ref[...]
    seg = row % 4
    plane_rows = KY * KX // CELLS
    depth = slab_ref[...] * (Z // SLABS) + row // plane_rows
    line = row // (KX // CELLS) % KY
    index = jnp.concatenate([depth, line], axis=0).astype(jnp.float32)
    own = jnp.where(seg == 0, every[0:32], every[32:64])
    own = jnp.where(seg == 2, every[64:96], own)
    own = jnp.where(seg == 3, every[96:128], own)
    sent = jnp.concatenate(
        [own.reshape(XW, 2, STEP), jnp.broadcast_to(index[None], (XW, 2, STEP))], axis=1
    )
    out_ref[...] = sent.astype(jnp.bfloat16)


def grid_blocks(pos_t, count, row, slab, samples, table, first, blocks):
    skip = first // STEP
    return pl.pallas_call(
        grid_kernel,
        grid=(blocks // STEP,),
        in_specs=[
            pl.BlockSpec((CELLS, STEP), lambda i: (0, i + skip)),
            pl.BlockSpec((1, STEP), lambda i: (0, i + skip)),
            pl.BlockSpec((1, STEP), lambda i: (0, i + skip)),
            pl.BlockSpec((1, STEP), lambda i: (0, i + skip)),
            pl.BlockSpec((STEP, 128), lambda i: (i + skip, 0)),
            pl.BlockSpec((128, 256), lambda i: (0, 0)),
        ],
        out_specs=pl.BlockSpec((XW, 4, STEP), lambda i: (0, 0, i)),
        out_shape=jax.ShapeDtypeStruct((XW, 4, blocks), jnp.bfloat16),
        scratch_shapes=[pltpu.VMEM((STEP, 128), jnp.float32), pltpu.VMEM((STEP, 256), jnp.bfloat16)],
        compiler_params=pltpu.CompilerParams(vmem_limit_bytes=60 * 1024 * 1024),
        cost_estimate=pl.CostEstimate(
            flops=4 * blocks * CELLS * 16 * CELLS, bytes_accessed=8 * blocks * CELLS, transcendentals=0
        ),
        name="grid_blocks",
    )(pos_t, count, row, slab, samples, table)


def place_step(values_ref, acc):
    sources, _, length = values_ref.shape
    iota = lax.broadcasted_iota(jnp.int32, (256, length), 0).astype(jnp.float32).astype(jnp.bfloat16)
    one = jnp.ones((), jnp.bfloat16)
    zero = jnp.zeros((), jnp.bfloat16)
    planes, spread = [], []
    for i in range(sources):
        rows = values_ref[i]
        planes.append(jnp.where(iota == rows[2:3], one, zero))
        hit = iota == rows[3:4]
        both = [jnp.where(hit, rows[p : p + 1], zero) for p in range(2)]
        spread.append(jnp.concatenate(both, axis=0))
    acc[...] += lax.dot_general(
        jnp.concatenate(spread, axis=1),
        jnp.concatenate(planes, axis=1),
        NT,
        preferred_element_type=jnp.float32,
    )


def place_first_kernel(values_ref, acc_ref):
    @pl.when(pl.program_id(0) == 0)
    def _():
        acc_ref[...] = jnp.zeros_like(acc_ref)

    place_step(values_ref, acc_ref)


def place_last_kernel(values_ref, start_ref, y_ref, z_ref, out_ref, acc):
    @pl.when(pl.program_id(0) == 0)
    def _():
        acc[...] = start_ref[...]

    place_step(values_ref, acc)

    @pl.when(pl.program_id(0) == pl.num_programs(0) - 1)
    def _():
        x_rows = acc[...].astype(jnp.bfloat16)
        y_t = jnp.dot(y_ref[...], x_rows, preferred_element_type=jnp.float32).astype(jnp.bfloat16)
        real, imag = y_t[0:256], y_t[256:512]

        def turn(table, side):
            return lax.dot_general(table, side, NT, preferred_element_type=jnp.float32)

        out_ref[:, 0:256] = (turn(z_ref[0], real) + turn(z_ref[2], imag)).astype(jnp.bfloat16)
        out_ref[:, 256:512] = (turn(z_ref[1], real) + turn(z_ref[0], imag)).astype(jnp.bfloat16)


def place_cost(values):
    sources, _, blocks = values.shape
    return pl.CostEstimate(
        flops=4 * sources * blocks * KY * Z, bytes_accessed=8 * sources * blocks, transcendentals=0
    )


def place_first(values):
    sources, rows, blocks = values.shape
    return pl.pallas_call(
        place_first_kernel,
        grid=(sources // TOGETHER,),
        in_specs=[pl.BlockSpec((TOGETHER, rows, blocks), lambda i: (i, 0, 0))],
        out_specs=pl.BlockSpec((2 * KY, Z), lambda i: (0, 0)),
        out_shape=jax.ShapeDtypeStruct((2 * KY, Z), jnp.float32),
        compiler_params=pltpu.CompilerParams(vmem_limit_bytes=50 * 1024 * 1024),
        cost_estimate=place_cost(values),
        name="place_first",
    )(values)


def place_last(values, start, y_table, z_tables):
    sources, rows, blocks = values.shape
    return pl.pallas_call(
        place_last_kernel,
        grid=(sources // TOGETHER,),
        in_specs=[
            pl.BlockSpec((TOGETHER, rows, blocks), lambda i: (i, 0, 0)),
            pl.BlockSpec((2 * KY, Z), lambda i: (0, 0)),
            pl.BlockSpec((2 * KY, 2 * KY), lambda i: (0, 0)),
            pl.BlockSpec((3, Z, Z), lambda i: (0, 0, 0)),
        ],
        out_specs=pl.BlockSpec((Z, 2 * KY), lambda i: (0, 0)),
        out_shape=jax.ShapeDtypeStruct((Z, 2 * KY), jnp.bfloat16),
        scratch_shapes=[pltpu.VMEM((2 * KY, Z), jnp.float32)],
        compiler_params=pltpu.CompilerParams(vmem_limit_bytes=50 * 1024 * 1024),
        cost_estimate=place_cost(values),
        name="place_last",
    )(values, start, y_table, z_tables)


def per_device(samples, sample_pos, block_count, grid_block, block_slab, sensitivity):
    slabs = lax.axis_size("slab")
    groups = lax.axis_size("coil")
    blocks = samples.shape[1]
    planes = sensitivity.shape[1]
    coils = sensitivity.shape[0]
    width = sensitivity.shape[2]
    table = jnp.asarray(across_table(), jnp.bfloat16)
    half = blocks // 2
    sent = []
    for part in range(2):
        sent.append(
            grid_blocks(
                sample_pos.T,
                block_count[None],
                grid_block[None],
                block_slab.reshape(1, blocks),
                samples[0],
                table,
                part * half,
                half,
            )
        )
    early = lax.all_to_all(sent[0], "slab", split_axis=0, concat_axis=0, tiled=True)
    early, later = lax.optimization_barrier((early, sent[1]))
    later = lax.all_to_all(later, "slab", split_axis=0, concat_axis=0, tiled=True)
    whole = place_last(
        later,
        place_first(early),
        jnp.asarray(line_table(KY), jnp.bfloat16),
        jnp.asarray(depth_tables(Z), jnp.bfloat16),
    )
    whole = whole.reshape(slabs, planes, 2 * KY)
    own = lax.all_to_all(whole, "slab", split_axis=0, concat_axis=0, tiled=True)
    own = own.reshape(groups, width, planes, 2 * KY)
    own = lax.all_to_all(own, "coil", split_axis=0, concat_axis=0, tiled=True)
    own = jnp.swapaxes(own.reshape(coils, width, planes, 2 * KY), 1, 2).astype(jnp.float32)
    maps = sensitivity.astype(jnp.float32)
    map_re, map_im = maps[..., :KY], maps[..., KY:]
    img_re, img_im = own[..., :KY], own[..., KY:]
    real_part = jnp.sum(map_re * img_re + map_im * img_im, axis=0)
    imag_part = jnp.sum(map_re * img_im - map_im * img_re, axis=0)
    return jnp.concatenate([real_part, imag_part], axis=-1)


def solution(mesh):
    return jax.shard_map(
        per_device,
        mesh=mesh,
        in_specs=(
            P("coil", "slab", None),
            P("slab", None),
            P("slab"),
            P("slab"),
            P("slab", None),
            P(None, "slab", "coil", None),
        ),
        out_specs=P("slab", "coil", None),
        check_vma=False,
    )
```

```python
import functools
import math

import jax
import jax.numpy as jnp
import numpy as np
from jax import lax
from jax.experimental import pallas as pl
from jax.experimental.pallas import tpu as pltpu
from jax.sharding import PartitionSpec as P

KX = 256
KY = 256
Z = 256
XW = 16
CELLS = 64
SLABS = 16
STEP = 2048
TOGETHER = 8
NT = (((1,), (1,)), ((), ()))


def twiddle(first, second, length):
    phase = (first * second % length).astype(np.float32) * np.float32(2.0 * math.pi / length)
    scale = 1.0 / math.sqrt(length)
    return np.cos(phase) * scale, np.sin(phase) * scale


def across_table():
    cell = np.arange(CELLS)
    rows = (KX - XW) // 2 + np.arange(XW)
    table = np.zeros((KX // CELLS, XW, 2, 2, 2, CELLS), np.float32)
    for s in range(KX // CELLS):
        cosine, sine = twiddle((s * CELLS + cell)[None, :], rows[:, None], KX)
        table[s, :, 0, 0] = cosine[:, None, :]
        table[s, :, 1, 0] = sine[:, None, :]
        table[s, :, 0, 1] = -sine[:, None, :]
        table[s, :, 1, 1] = cosine[:, None, :]
    return table.reshape(KX // CELLS * XW * 2, 4 * CELLS)


def line_table(length):
    index = np.arange(length)
    cosine, sine = twiddle(index[:, None], index[None, :], length)
    return np.block([[cosine, -sine], [sine, cosine]])


def depth_tables(length):
    index = np.arange(length)
    cosine, sine = twiddle(index[:, None], index[None, :], length)
    return np.stack([cosine, sine, -sine])


def grid_kernel(pos_ref, count_ref, row_ref, slab_ref, samples_ref, table_ref, out_ref, pos_s, g_s):
    tiles = STEP // 32
    sample = lax.broadcasted_iota(jnp.int32, (CELLS, STEP), 0)
    live = sample < count_ref[...]
    pos = jnp.where(live, pos_ref[...].astype(jnp.float32) * 0.4, -100.0)
    pos_s[:, 0:CELLS] = pos.T
    mids = (lax.broadcasted_iota(jnp.int32, (CELLS, 256), 0).astype(jnp.float32) + 0.5) * 0.4
    low = lax.broadcasted_iota(jnp.int32, (8, 128), 1) < 64
    sub = lax.broadcasted_iota(jnp.int32, (32, 128), 0) % 8
    lane_half = lax.broadcasted_iota(jnp.int32, (32, 128), 1) // 64
    keep = lane_half == sub % 2
    group = sub // 2

    def one_tile(t, carry):
        start = pl.multiple_of(t * 32, 32)
        pos_rows = pos_s[pl.ds(start, 32), :]
        halves = []
        for h in range(2):
            even = pos_rows[16 * h : 16 * h + 8]
            odd = pltpu.roll(pos_rows[16 * h + 8 : 16 * h + 16], 64, 1)
            halves.append(jnp.where(low, even, odd))
        row4 = jnp.concatenate(halves, axis=1)
        parts = []
        for nb in range(8):
            offset = row4[nb : nb + 1, :] - mids
            bump = jnp.maximum(1.0 - offset * offset, 0.0)
            parts.append((bump * bump).astype(jnp.bfloat16))
        weights = jnp.concatenate(parts, axis=0)
        vals = samples_ref[pl.ds(start, 32), :].astype(jnp.float32)
        zero = jnp.zeros((8, 128), jnp.float32)
        lhs = []
        for p in range(2):
            for kb in range(4):
                piece = vals[8 * kb : 8 * kb + 8]
                if kb % 2 != p:
                    piece = pltpu.roll(piece, 64, 1)
                piece = jnp.where(low == (kb % 2 == 0), piece, 0.0)
                lhs.append(jnp.concatenate([piece, zero] if kb < 2 else [zero, piece], axis=1))
        lhs = jnp.concatenate(lhs, axis=0).astype(jnp.bfloat16)
        full = lax.dot_general(lhs, weights, NT, preferred_element_type=jnp.float32)
        sides = []
        for p in range(2):
            block = full[32 * p : 32 * p + 32]
            own = jnp.where(group == 0, block[:, 0:128], block[:, 128:256])
            own = jnp.where(group == 2, block[:, 256:384], own)
            own = jnp.where(group == 3, block[:, 384:512], own)
            sides.append(jnp.where(keep, own, 0.0))
        g_s[pl.ds(start, 32), :] = jnp.concatenate(sides, axis=1).astype(jnp.bfloat16)
        return carry

    lax.fori_loop(0, tiles, one_tile, 0, unroll=True)
    every = lax.dot_general(table_ref[...], g_s[...], NT, preferred_element_type=jnp.float32)
    row = row_ref[...]
    seg = row % 4
    plane_rows = KY * KX // CELLS
    depth = slab_ref[...] * (Z // SLABS) + row // plane_rows
    line = row // (KX // CELLS) % KY
    index = jnp.concatenate([depth, line], axis=0).astype(jnp.float32)
    own = jnp.where(seg == 0, every[0:32], every[32:64])
    own = jnp.where(seg == 2, every[64:96], own)
    own = jnp.where(seg == 3, every[96:128], own)
    sent = jnp.concatenate(
        [own.reshape(XW, 2, STEP), jnp.broadcast_to(index[None], (XW, 2, STEP))], axis=1
    )
    out_ref[...] = sent.astype(jnp.bfloat16)


def grid_blocks(pos_t, count, row, slab, samples, table, first, blocks):
    skip = first // STEP
    return pl.pallas_call(
        grid_kernel,
        grid=(blocks // STEP,),
        in_specs=[
            pl.BlockSpec((CELLS, STEP), lambda i: (0, i + skip)),
            pl.BlockSpec((1, STEP), lambda i: (0, i + skip)),
            pl.BlockSpec((1, STEP), lambda i: (0, i + skip)),
            pl.BlockSpec((1, STEP), lambda i: (0, i + skip)),
            pl.BlockSpec((STEP, 128), lambda i: (i + skip, 0)),
            pl.BlockSpec((128, 256), lambda i: (0, 0)),
        ],
        out_specs=pl.BlockSpec((XW, 4, STEP), lambda i: (0, 0, i)),
        out_shape=jax.ShapeDtypeStruct((XW, 4, blocks), jnp.bfloat16),
        scratch_shapes=[pltpu.VMEM((STEP, 128), jnp.float32), pltpu.VMEM((STEP, 256), jnp.bfloat16)],
        compiler_params=pltpu.CompilerParams(vmem_limit_bytes=60 * 1024 * 1024),
        cost_estimate=pl.CostEstimate(
            flops=4 * blocks * CELLS * 16 * CELLS, bytes_accessed=8 * blocks * CELLS, transcendentals=0
        ),
        name="grid_blocks",
    )(pos_t, count, row, slab, samples, table)


def place_step(values_ref, acc):
    sources, _, length = values_ref.shape
    iota = lax.broadcasted_iota(jnp.int32, (256, length), 0).astype(jnp.float32).astype(jnp.bfloat16)
    one = jnp.ones((), jnp.bfloat16)
    zero = jnp.zeros((), jnp.bfloat16)
    planes, spread = [], []
    for i in range(sources):
        rows = values_ref[i]
        planes.append(jnp.where(iota == rows[2:3], one, zero))
        hit = iota == rows[3:4]
        both = [jnp.where(hit, rows[p : p + 1], zero) for p in range(2)]
        spread.append(jnp.concatenate(both, axis=0))
    acc[...] += lax.dot_general(
        jnp.concatenate(spread, axis=1),
        jnp.concatenate(planes, axis=1),
        NT,
        preferred_element_type=jnp.float32,
    )


def place_first_kernel(values_ref, acc_ref):
    @pl.when(pl.program_id(0) == 0)
    def _():
        acc_ref[...] = jnp.zeros_like(acc_ref)

    place_step(values_ref, acc_ref)


def place_last_kernel(values_ref, start_ref, y_ref, z_ref, out_ref, acc):
    @pl.when(pl.program_id(0) == 0)
    def _():
        acc[...] = start_ref[...]

    place_step(values_ref, acc)

    @pl.when(pl.program_id(0) == pl.num_programs(0) - 1)
    def _():
        x_rows = acc[...].astype(jnp.bfloat16)
        y_t = jnp.dot(y_ref[...], x_rows, preferred_element_type=jnp.float32).astype(jnp.bfloat16)
        real, imag = y_t[0:256], y_t[256:512]

        def turn(table, side):
            return lax.dot_general(table, side, NT, preferred_element_type=jnp.float32)

        out_ref[:, 0:256] = (turn(z_ref[0], real) + turn(z_ref[2], imag)).astype(jnp.bfloat16)
        out_ref[:, 256:512] = (turn(z_ref[1], real) + turn(z_ref[0], imag)).astype(jnp.bfloat16)


def place_cost(values):
    sources, _, blocks = values.shape
    return pl.CostEstimate(
        flops=4 * sources * blocks * KY * Z, bytes_accessed=8 * sources * blocks, transcendentals=0
    )


def place_first(values):
    sources, rows, blocks = values.shape
    return pl.pallas_call(
        place_first_kernel,
        grid=(sources // TOGETHER,),
        in_specs=[pl.BlockSpec((TOGETHER, rows, blocks), lambda i: (i, 0, 0))],
        out_specs=pl.BlockSpec((2 * KY, Z), lambda i: (0, 0)),
        out_shape=jax.ShapeDtypeStruct((2 * KY, Z), jnp.float32),
        compiler_params=pltpu.CompilerParams(vmem_limit_bytes=50 * 1024 * 1024),
        cost_estimate=place_cost(values),
        name="place_first",
    )(values)


def place_last(values, start, y_table, z_tables):
    sources, rows, blocks = values.shape
    return pl.pallas_call(
        place_last_kernel,
        grid=(sources // TOGETHER,),
        in_specs=[
            pl.BlockSpec((TOGETHER, rows, blocks), lambda i: (i, 0, 0)),
            pl.BlockSpec((2 * KY, Z), lambda i: (0, 0)),
            pl.BlockSpec((2 * KY, 2 * KY), lambda i: (0, 0)),
            pl.BlockSpec((3, Z, Z), lambda i: (0, 0, 0)),
        ],
        out_specs=pl.BlockSpec((Z, 2 * KY), lambda i: (0, 0)),
        out_shape=jax.ShapeDtypeStruct((Z, 2 * KY), jnp.bfloat16),
        scratch_shapes=[pltpu.VMEM((2 * KY, Z), jnp.float32)],
        compiler_params=pltpu.CompilerParams(vmem_limit_bytes=50 * 1024 * 1024),
        cost_estimate=place_cost(values),
        name="place_last",
    )(values, start, y_table, z_tables)


def per_device(samples, sample_pos, block_count, grid_block, block_slab, sensitivity):
    slabs = lax.axis_size("slab")
    groups = lax.axis_size("coil")
    blocks = samples.shape[1]
    planes = sensitivity.shape[1]
    coils = sensitivity.shape[0]
    width = sensitivity.shape[2]
    table = jnp.asarray(across_table(), jnp.bfloat16)
    half = blocks // 2
    sent = []
    for part in range(2):
        sent.append(
            grid_blocks(
                sample_pos.T,
                block_count[None],
                grid_block[None],
                block_slab.reshape(1, blocks),
                samples[0],
                table,
                part * half,
                half,
            )
        )
    early = lax.all_to_all(sent[0], "slab", split_axis=0, concat_axis=0, tiled=True)
    early, later = lax.optimization_barrier((early, sent[1]))
    later = lax.all_to_all(later, "slab", split_axis=0, concat_axis=0, tiled=True)
    whole = place_last(
        later,
        place_first(early),
        jnp.asarray(line_table(KY), jnp.bfloat16),
        jnp.asarray(depth_tables(Z), jnp.bfloat16),
    )
    whole = whole.reshape(slabs, planes, 2 * KY)
    own = lax.all_to_all(whole, "slab", split_axis=0, concat_axis=0, tiled=True)
    whole, half_maps = lax.optimization_barrier((whole, sensitivity[..., :KY]))
    map_re = half_maps.astype(jnp.float32)
    own, map_re, half_maps = lax.optimization_barrier((own, map_re, sensitivity[..., KY:]))
    own = own.reshape(groups, width, planes, 2 * KY)
    own = lax.all_to_all(own, "coil", split_axis=0, concat_axis=0, tiled=True)
    own, map_im = lax.optimization_barrier((own, half_maps.astype(jnp.float32)))
    own = jnp.swapaxes(own.reshape(coils, width, planes, 2 * KY), 1, 2).astype(jnp.float32)
    img_re, img_im = own[..., :KY], own[..., KY:]
    real_part = jnp.sum(map_re * img_re + map_im * img_im, axis=0)
    imag_part = jnp.sum(map_re * img_im - map_im * img_re, axis=0)
    return jnp.concatenate([real_part, imag_part], axis=-1)


def solution(mesh):
    return jax.shard_map(
        per_device,
        mesh=mesh,
        in_specs=(
            P("coil", "slab", None),
            P("slab", None),
            P("slab"),
            P("slab"),
            P("slab", None),
            P(None, "slab", "coil", None),
        ),
        out_specs=P("slab", "coil", None),
        check_vma=False,
    )
```

```python
import functools
import math

import jax
import jax.numpy as jnp
import numpy as np
from jax import lax
from jax.experimental import pallas as pl
from jax.experimental.pallas import tpu as pltpu
from jax.sharding import PartitionSpec as P

KX = 256
KY = 256
Z = 256
XW = 16
CELLS = 64
SLABS = 16
STEP = 2048
NT = (((1,), (1,)), ((), ()))


def twiddle(first, second, length):
    phase = (first * second % length).astype(np.float32) * np.float32(2.0 * math.pi / length)
    scale = 1.0 / math.sqrt(length)
    return np.cos(phase) * scale, np.sin(phase) * scale


def across_table():
    cell = np.arange(CELLS)
    rows = (KX - XW) // 2 + np.arange(XW)
    table = np.zeros((KX // CELLS, 2, CELLS, 2, XW), np.float32)
    for s in range(KX // CELLS):
        cosine, sine = twiddle((s * CELLS + cell)[:, None], rows[None, :], KX)
        table[s, 0, :, 0] = cosine
        table[s, 0, :, 1] = sine
        table[s, 1, :, 0] = -sine
        table[s, 1, :, 1] = cosine
    return table.reshape(2 * KX, 2 * XW)


def line_table(length):
    index = np.arange(length)
    cosine, sine = twiddle(index[:, None], index[None, :], length)
    return np.block([[cosine, -sine], [sine, cosine]])


def depth_tables(length):
    index = np.arange(length)
    cosine, sine = twiddle(index[:, None], index[None, :], length)
    return np.stack([cosine, sine, -sine])


def grid_kernel(pos_ref, count_ref, samples_ref, out_ref, pos_s):
    tiles = STEP // 32
    sample = lax.broadcasted_iota(jnp.int32, (CELLS, STEP), 0)
    live = sample < count_ref[...]
    pos = jnp.where(live, pos_ref[...].astype(jnp.float32) * 0.4, -100.0)
    pos_s[:, 0:CELLS] = pos.T
    mids = (lax.broadcasted_iota(jnp.int32, (CELLS, 256), 0).astype(jnp.float32) + 0.5) * 0.4
    low = lax.broadcasted_iota(jnp.int32, (8, 128), 1) < 64
    sub = lax.broadcasted_iota(jnp.int32, (32, 128), 0) % 8
    lane_half = lax.broadcasted_iota(jnp.int32, (32, 128), 1) // 64
    keep = lane_half == sub % 2
    group = sub // 2

    def one_tile(t, carry):
        start = pl.multiple_of(t * 32, 32)
        pos_rows = pos_s[pl.ds(start, 32), :]
        halves = []
        for h in range(2):
            even = pos_rows[16 * h : 16 * h + 8]
            odd = pltpu.roll(pos_rows[16 * h + 8 : 16 * h + 16], 64, 1)
            halves.append(jnp.where(low, even, odd))
        row4 = jnp.concatenate(halves, axis=1)
        parts = []
        for nb in range(8):
            offset = row4[nb : nb + 1, :] - mids
            bump = jnp.maximum(1.0 - offset * offset, 0.0)
            parts.append((bump * bump).astype(jnp.bfloat16))
        weights = jnp.concatenate(parts, axis=0)
        vals = samples_ref[pl.ds(start, 32), :].astype(jnp.float32)
        zero = jnp.zeros((8, 128), jnp.float32)
        lhs = []
        for p in range(2):
            for kb in range(4):
                piece = vals[8 * kb : 8 * kb + 8]
                if kb % 2 != p:
                    piece = pltpu.roll(piece, 64, 1)
                piece = jnp.where(low == (kb % 2 == 0), piece, 0.0)
                lhs.append(jnp.concatenate([piece, zero] if kb < 2 else [zero, piece], axis=1))
        lhs = jnp.concatenate(lhs, axis=0).astype(jnp.bfloat16)
        full = lax.dot_general(lhs, weights, NT, preferred_element_type=jnp.float32)
        sides = []
        for p in range(2):
            block = full[32 * p : 32 * p + 32]
            own = jnp.where(group == 0, block[:, 0:128], block[:, 128:256])
            own = jnp.where(group == 2, block[:, 256:384], own)
            own = jnp.where(group == 3, block[:, 384:512], own)
            own = jnp.where(keep, own, 0.0)
            sides.append(own + pltpu.roll(own, 64, 1))
        out_ref[pl.ds(start, 32), :] = jnp.where(lane_half == 0, sides[0], sides[1]).astype(jnp.bfloat16)
        return carry

    lax.fori_loop(0, tiles, one_tile, 0, unroll=True)


def grid_blocks(pos_t, count, samples):
    blocks = samples.shape[0]
    return pl.pallas_call(
        grid_kernel,
        grid=(blocks // STEP,),
        in_specs=[
            pl.BlockSpec((CELLS, STEP), lambda i: (0, i)),
            pl.BlockSpec((1, STEP), lambda i: (0, i)),
            pl.BlockSpec((STEP, 128), lambda i: (i, 0)),
        ],
        out_specs=pl.BlockSpec((STEP, 128), lambda i: (i, 0)),
        out_shape=jax.ShapeDtypeStruct((blocks, 128), jnp.bfloat16),
        scratch_shapes=[pltpu.VMEM((STEP, 128), jnp.float32)],
        compiler_params=pltpu.CompilerParams(vmem_limit_bytes=60 * 1024 * 1024),
        name="grid_blocks",
    )(pos_t, count, samples)


def add_kernel(rows_ref, values_ref, out_ref, acc):
    step = pl.program_id(0)
    length = values_ref.shape[0]

    @pl.when(step == 0)
    def _():
        acc[...] = jnp.zeros_like(acc)

    def some(i, carry):
        start = pl.multiple_of(i * 16, 16)
        values = values_ref[pl.ds(start, 16), :].astype(jnp.float32)
        for q in range(16):
            row = rows_ref[step * length + start + q]
            acc[pl.ds(row, 1), :] += values[q : q + 1]
        return carry

    lax.fori_loop(0, length // 16, some, 0, unroll=2)

    @pl.when(step == pl.num_programs(0) - 1)
    def _():
        out_ref[...] = acc[...].astype(jnp.bfloat16)


def add_rows(rows, values, total):
    slots = values.shape[0]
    return pl.pallas_call(
        add_kernel,
        grid_spec=pltpu.PrefetchScalarGridSpec(
            num_scalar_prefetch=1,
            grid=(slots // STEP,),
            in_specs=[pl.BlockSpec((STEP, 128), lambda i, rows: (i, 0))],
            out_specs=pl.BlockSpec((total, 128), lambda i, rows: (0, 0)),
            scratch_shapes=[pltpu.VMEM((total, 128), jnp.float32)],
        ),
        out_shape=jax.ShapeDtypeStruct((total, 128), jnp.bfloat16),
        compiler_params=pltpu.CompilerParams(vmem_limit_bytes=48 * 1024 * 1024),
        name="add_rows",
    )(rows, values)


def slots_of(slab, slabs, capacity):
    hot = slab[:, None] == jnp.arange(slabs, dtype=jnp.int32)[None, :]
    chunks = hot.reshape(-1, 128, slabs).astype(jnp.float32)
    inner = jnp.asarray(np.tril(np.ones((128, 128)), -1), jnp.float32)
    outer = jnp.asarray(np.tril(np.ones((chunks.shape[0], chunks.shape[0])), -1), jnp.float32)
    exact = lax.Precision.HIGHEST
    before = jnp.einsum("ij,cjs->cis", inner, chunks, precision=exact)
    before += jnp.einsum("cd,ds->cs", outer, jnp.sum(chunks, axis=1), precision=exact)[:, None]
    rank = jnp.sum(before * chunks, axis=2).reshape(-1)
    return slab * capacity + (rank + 0.5).astype(jnp.int32)


def per_device(samples, sample_pos, block_count, grid_block, block_slab, sensitivity):
    slabs = lax.axis_size("slab")
    groups = lax.axis_size("coil")
    blocks = samples.shape[1]
    planes = sensitivity.shape[1]
    coils = sensitivity.shape[0]
    width = sensitivity.shape[2]
    capacity = 5 * blocks // (2 * slabs)
    slot = slots_of(block_slab[:, 0], slabs, capacity)
    target = jnp.zeros((slabs * capacity,), jnp.int32).at[slot].set(grid_block)
    target = target.reshape(slabs, capacity // 128, 128)
    target = lax.all_to_all(target, "slab", split_axis=0, concat_axis=0, tiled=True)
    gridded = grid_blocks(sample_pos.T, block_count[None], samples[0])
    packed = jnp.zeros((slabs * capacity, 128), jnp.bfloat16).at[slot].set(gridded)
    packed = packed.reshape(slabs, capacity, 128)
    packed = lax.all_to_all(packed, "slab", split_axis=0, concat_axis=0, tiled=True)
    kspace = add_rows(target.reshape(-1), packed.reshape(-1, 128), planes * KY * KX // CELLS)
    x_rows = jnp.dot(
        kspace.reshape(planes * KY, 2 * KX),
        jnp.asarray(across_table(), jnp.bfloat16),
        preferred_element_type=jnp.float32,
    ).astype(jnp.bfloat16)
    y_planes = jnp.einsum(
        "zkqx,qkn->zxn",
        x_rows.reshape(planes, KY, 2, XW),
        jnp.asarray(line_table(KY).T.reshape(2, KY, 2 * KY), jnp.bfloat16),
        preferred_element_type=jnp.float32,
    ).astype(jnp.bfloat16)
    lines = lax.all_to_all(y_planes, "slab", split_axis=1, concat_axis=0, tiled=True)
    lines = lines.reshape(Z, 2, KY)
    turns = jnp.asarray(depth_tables(Z), jnp.bfloat16)
    turns = jnp.stack([jnp.stack([turns[0], turns[2]]), jnp.stack([turns[1], turns[0]])])
    whole = jnp.einsum("pqzk,kqy->zpy", turns, lines, preferred_element_type=jnp.float32)
    whole = whole.astype(jnp.bfloat16).reshape(slabs, planes, 2 * KY)
    own = lax.all_to_all(whole, "slab", split_axis=0, concat_axis=0, tiled=True)
    whole, half_maps = lax.optimization_barrier((whole, sensitivity[..., :KY]))
    map_re = half_maps.astype(jnp.float32)
    own, map_re, half_maps = lax.optimization_barrier((own, map_re, sensitivity[..., KY:]))
    own = own.reshape(groups, width, planes, 2 * KY)
    own = lax.all_to_all(own, "coil", split_axis=0, concat_axis=0, tiled=True)
    own, map_im = lax.optimization_barrier((own, half_maps.astype(jnp.float32)))
    own = jnp.swapaxes(own.reshape(coils, width, planes, 2 * KY), 1, 2).astype(jnp.float32)
    img_re, img_im = own[..., :KY], own[..., KY:]
    real_part = jnp.sum(map_re * img_re + map_im * img_im, axis=0)
    imag_part = jnp.sum(map_re * img_im - map_im * img_re, axis=0)
    return jnp.concatenate([real_part, imag_part], axis=-1)


def solution(mesh):
    return jax.shard_map(
        per_device,
        mesh=mesh,
        in_specs=(
            P("coil", "slab", None),
            P("slab", None),
            P("slab"),
            P("slab"),
            P("slab", None),
            P(None, "slab", "coil", None),
        ),
        out_specs=P("slab", "coil", None),
        check_vma=False,
    )
```

```python
import functools
import math

import jax
import jax.numpy as jnp
import numpy as np
from jax import lax
from jax.experimental import pallas as pl
from jax.experimental.pallas import tpu as pltpu
from jax.sharding import PartitionSpec as P

KX = 256
KY = 256
Z = 256
XW = 16
CELLS = 64
SLABS = 16
STEP = 2048
ADDED = 1024
LANES = 4
NT = (((1,), (1,)), ((), ()))


def twiddle(first, second, length):
    phase = (first * second % length).astype(np.float32) * np.float32(2.0 * math.pi / length)
    scale = 1.0 / math.sqrt(length)
    return np.cos(phase) * scale, np.sin(phase) * scale


def across_table():
    cell = np.arange(CELLS)
    rows = (KX - XW) // 2 + np.arange(XW)
    table = np.zeros((KX // CELLS, 2, CELLS, 2, XW), np.float32)
    for s in range(KX // CELLS):
        cosine, sine = twiddle((s * CELLS + cell)[:, None], rows[None, :], KX)
        table[s, 0, :, 0] = cosine
        table[s, 0, :, 1] = sine
        table[s, 1, :, 0] = -sine
        table[s, 1, :, 1] = cosine
    return table.reshape(2 * KX, 2 * XW)


def line_table(length):
    index = np.arange(length)
    cosine, sine = twiddle(index[:, None], index[None, :], length)
    return np.block([[cosine, -sine], [sine, cosine]])


def depth_tables(length):
    index = np.arange(length)
    cosine, sine = twiddle(index[:, None], index[None, :], length)
    return np.stack([cosine, sine, -sine])


def grid_kernel(pos_ref, count_ref, samples_ref, out_ref, pos_s):
    tiles = STEP // 32
    sample = lax.broadcasted_iota(jnp.int32, (CELLS, STEP), 0)
    live = sample < count_ref[...]
    pos = jnp.where(live, pos_ref[...].astype(jnp.float32) * 0.4, -100.0)
    pos_s[:, 0:CELLS] = pos.T
    mids = (lax.broadcasted_iota(jnp.int32, (CELLS, 256), 0).astype(jnp.float32) + 0.5) * 0.4
    low = lax.broadcasted_iota(jnp.int32, (8, 128), 1) < 64
    sub = lax.broadcasted_iota(jnp.int32, (32, 128), 0) % 8
    lane_half = lax.broadcasted_iota(jnp.int32, (32, 128), 1) // 64
    keep = lane_half == sub % 2
    group = sub // 2

    def one_tile(t, carry):
        start = pl.multiple_of(t * 32, 32)
        pos_rows = pos_s[pl.ds(start, 32), :]
        halves = []
        for h in range(2):
            even = pos_rows[16 * h : 16 * h + 8]
            odd = pltpu.roll(pos_rows[16 * h + 8 : 16 * h + 16], 64, 1)
            halves.append(jnp.where(low, even, odd))
        row4 = jnp.concatenate(halves, axis=1)
        parts = []
        for nb in range(8):
            offset = row4[nb : nb + 1, :] - mids
            bump = jnp.maximum(1.0 - offset * offset, 0.0)
            parts.append((bump * bump).astype(jnp.bfloat16))
        weights = jnp.concatenate(parts, axis=0)
        vals = samples_ref[pl.ds(start, 32), :].astype(jnp.float32)
        zero = jnp.zeros((8, 128), jnp.float32)
        lhs = []
        for p in range(2):
            for kb in range(4):
                piece = vals[8 * kb : 8 * kb + 8]
                if kb % 2 != p:
                    piece = pltpu.roll(piece, 64, 1)
                piece = jnp.where(low == (kb % 2 == 0), piece, 0.0)
                lhs.append(jnp.concatenate([piece, zero] if kb < 2 else [zero, piece], axis=1))
        lhs = jnp.concatenate(lhs, axis=0).astype(jnp.bfloat16)
        full = lax.dot_general(lhs, weights, NT, preferred_element_type=jnp.float32)
        sides = []
        for p in range(2):
            block = full[32 * p : 32 * p + 32]
            own = jnp.where(group == 0, block[:, 0:128], block[:, 128:256])
            own = jnp.where(group == 2, block[:, 256:384], own)
            own = jnp.where(group == 3, block[:, 384:512], own)
            own = jnp.where(keep, own, 0.0)
            sides.append(own + pltpu.roll(own, 64, 1))
        out_ref[pl.ds(start, 32), :] = jnp.where(lane_half == 0, sides[0], sides[1]).astype(jnp.bfloat16)
        return carry

    lax.fori_loop(0, tiles, one_tile, 0, unroll=True)


def grid_blocks(pos_t, count, samples):
    blocks = samples.shape[0]
    return pl.pallas_call(
        grid_kernel,
        grid=(blocks // STEP,),
        in_specs=[
            pl.BlockSpec((CELLS, STEP), lambda i: (0, i)),
            pl.BlockSpec((1, STEP), lambda i: (0, i)),
            pl.BlockSpec((STEP, 128), lambda i: (i, 0)),
        ],
        out_specs=pl.BlockSpec((STEP, 128), lambda i: (i, 0)),
        out_shape=jax.ShapeDtypeStruct((blocks, 128), jnp.bfloat16),
        scratch_shapes=[pltpu.VMEM((STEP, 128), jnp.float32)],
        compiler_params=pltpu.CompilerParams(vmem_limit_bytes=60 * 1024 * 1024),
        name="grid_blocks",
    )(pos_t, count, samples)


def pack_kernel(slot_ref, row_ref, zeros_ref, values_ref, out_ref, target_ref, wide):
    pltpu.sync_copy(zeros_ref, target_ref)
    wide[...] = jnp.zeros_like(wide)

    def some(i, carry):
        start = pl.multiple_of(i * 16, 16)
        values = values_ref[pl.ds(start, 16), :].astype(jnp.float32)
        for q in range(16):
            slot = slot_ref[start + q]
            wide[pl.ds(slot, 1), :] = values[q : q + 1]
            target_ref[slot] = row_ref[start + q]
        return carry

    lax.fori_loop(0, values_ref.shape[0] // 16, some, 0, unroll=2)
    out_ref[...] = wide[...].astype(jnp.bfloat16)


def pack_rows(slot, row, values, slots):
    blocks = values.shape[0]
    return pl.pallas_call(
        pack_kernel,
        grid_spec=pltpu.PrefetchScalarGridSpec(
            num_scalar_prefetch=2,
            grid=(1,),
            in_specs=[
                pl.BlockSpec(memory_space=pl.ANY),
                pl.BlockSpec((blocks, 128), lambda i, slot, row: (0, 0)),
            ],
            out_specs=[
                pl.BlockSpec((slots, 128), lambda i, slot, row: (0, 0)),
                pl.BlockSpec(memory_space=pltpu.SMEM),
            ],
            scratch_shapes=[pltpu.VMEM((slots, 128), jnp.float32)],
        ),
        out_shape=[
            jax.ShapeDtypeStruct((slots, 128), jnp.bfloat16),
            jax.ShapeDtypeStruct((slots,), jnp.int32),
        ],
        compiler_params=pltpu.CompilerParams(vmem_limit_bytes=48 * 1024 * 1024),
        name="pack_rows",
    )(slot, row, jnp.zeros((slots,), jnp.int32), values)


def add_kernel(rows_ref, *refs):
    values_refs, out_ref, accs = refs[:LANES], refs[LANES], refs[LANES + 1 :]
    step = pl.program_id(0)
    length = values_refs[0].shape[0]
    share = length * pl.num_programs(0)

    @pl.when(step == 0)
    def _():
        for acc in accs:
            acc[...] = jnp.zeros_like(acc)

    def some(i, carry):
        start = pl.multiple_of(i * 16, 16)
        values = [ref[pl.ds(start, 16), :].astype(jnp.float32) for ref in values_refs]
        for q in range(16):
            for n in range(LANES):
                row = rows_ref[n * share + step * length + start + q]
                accs[n][pl.ds(row, 1), :] += values[n][q : q + 1]
        return carry

    lax.fori_loop(0, length // 16, some, 0)

    @pl.when(step == pl.num_programs(0) - 1)
    def _():
        total = accs[0][...]
        for acc in accs[1:]:
            total = total + acc[...]
        out_ref[...] = total.astype(jnp.bfloat16)


def add_rows(rows, values, total):
    slots = values.shape[0]
    steps = slots // LANES // ADDED
    return pl.pallas_call(
        add_kernel,
        grid_spec=pltpu.PrefetchScalarGridSpec(
            num_scalar_prefetch=1,
            grid=(steps,),
            in_specs=[
                pl.BlockSpec((ADDED, 128), lambda i, rows, n=n: (n * steps + i, 0)) for n in range(LANES)
            ],
            out_specs=pl.BlockSpec((total, 128), lambda i, rows: (0, 0)),
            scratch_shapes=[pltpu.VMEM((total, 128), jnp.float32)] * LANES,
        ),
        out_shape=jax.ShapeDtypeStruct((total, 128), jnp.bfloat16),
        compiler_params=pltpu.CompilerParams(vmem_limit_bytes=58 * 1024 * 1024),
        name="add_rows",
    )(rows, *[values] * LANES)


def slots_of(slab, slabs, capacity):
    hot = slab[:, None] == jnp.arange(slabs, dtype=jnp.int32)[None, :]
    chunks = hot.reshape(-1, 128, slabs).astype(jnp.float32)
    inner = jnp.asarray(np.tril(np.ones((128, 128)), -1), jnp.float32)
    outer = jnp.asarray(np.tril(np.ones((chunks.shape[0], chunks.shape[0])), -1), jnp.float32)
    exact = lax.Precision.HIGHEST
    before = jnp.einsum("ij,cjs->cis", inner, chunks, precision=exact)
    before += jnp.einsum("cd,ds->cs", outer, jnp.sum(chunks, axis=1), precision=exact)[:, None]
    rank = jnp.sum(before * chunks, axis=2).reshape(-1)
    return slab * capacity + (rank + 0.5).astype(jnp.int32)


def per_device(samples, sample_pos, block_count, grid_block, block_slab, sensitivity):
    slabs = lax.axis_size("slab")
    groups = lax.axis_size("coil")
    blocks = samples.shape[1]
    planes = sensitivity.shape[1]
    coils = sensitivity.shape[0]
    width = sensitivity.shape[2]
    capacity = 5 * blocks // (2 * slabs)
    slot = slots_of(block_slab[:, 0], slabs, capacity)
    gridded = grid_blocks(sample_pos.T, block_count[None], samples[0])
    packed, target = pack_rows(slot, grid_block, gridded, slabs * capacity)
    packed = packed.reshape(slabs, capacity, 128)
    packed = lax.all_to_all(packed, "slab", split_axis=0, concat_axis=0, tiled=True)
    target = target.reshape(slabs, capacity // 128, 128)
    target = lax.all_to_all(target, "slab", split_axis=0, concat_axis=0, tiled=True)
    kspace = add_rows(target.reshape(-1), packed.reshape(-1, 128), planes * KY * KX // CELLS)
    x_rows = jnp.dot(
        kspace.reshape(planes * KY, 2 * KX),
        jnp.asarray(across_table(), jnp.bfloat16),
        preferred_element_type=jnp.float32,
    ).astype(jnp.bfloat16)
    y_planes = jnp.einsum(
        "zkqx,qkn->zxn",
        x_rows.reshape(planes, KY, 2, XW),
        jnp.asarray(line_table(KY).T.reshape(2, KY, 2 * KY), jnp.bfloat16),
        preferred_element_type=jnp.float32,
    ).astype(jnp.bfloat16)
    lines = lax.all_to_all(y_planes, "slab", split_axis=1, concat_axis=0, tiled=True)
    lines = lines.reshape(Z, 2, KY)
    turns = jnp.asarray(depth_tables(Z), jnp.bfloat16)
    turns = jnp.stack([jnp.stack([turns[0], turns[2]]), jnp.stack([turns[1], turns[0]])])
    whole = jnp.einsum("pqzk,kqy->zpy", turns, lines, preferred_element_type=jnp.float32)
    whole = whole.astype(jnp.bfloat16).reshape(slabs, planes, 2 * KY)
    own = lax.all_to_all(whole, "slab", split_axis=0, concat_axis=0, tiled=True)
    whole, half_maps = lax.optimization_barrier((whole, sensitivity[..., :KY]))
    map_re = half_maps.astype(jnp.float32)
    own, map_re, half_maps = lax.optimization_barrier((own, map_re, sensitivity[..., KY:]))
    own = own.reshape(groups, width, planes, 2 * KY)
    own = lax.all_to_all(own, "coil", split_axis=0, concat_axis=0, tiled=True)
    own, map_im = lax.optimization_barrier((own, half_maps.astype(jnp.float32)))
    own = jnp.swapaxes(own.reshape(coils, width, planes, 2 * KY), 1, 2).astype(jnp.float32)
    img_re, img_im = own[..., :KY], own[..., KY:]
    real_part = jnp.sum(map_re * img_re + map_im * img_im, axis=0)
    imag_part = jnp.sum(map_re * img_im - map_im * img_re, axis=0)
    return jnp.concatenate([real_part, imag_part], axis=-1)


def solution(mesh):
    return jax.shard_map(
        per_device,
        mesh=mesh,
        in_specs=(
            P("coil", "slab", None),
            P("slab", None),
            P("slab"),
            P("slab"),
            P("slab", None),
            P(None, "slab", "coil", None),
        ),
        out_specs=P("slab", "coil", None),
        check_vma=False,
    )
```

```python
import functools
import math

import jax
import jax.numpy as jnp
import numpy as np
from jax import lax
from jax.experimental import pallas as pl
from jax.experimental.pallas import tpu as pltpu
from jax.sharding import PartitionSpec as P

KX = 256
KY = 256
Z = 256
XW = 16
CELLS = 64
SLABS = 16
STEP = 2048
ADDED = 1024
LANES = 4
NT = (((1,), (1,)), ((), ()))


def twiddle(first, second, length):
    phase = (first * second % length).astype(np.float32) * np.float32(2.0 * math.pi / length)
    scale = 1.0 / math.sqrt(length)
    return np.cos(phase) * scale, np.sin(phase) * scale


def across_table():
    cell = np.arange(CELLS)
    rows = (KX - XW) // 2 + np.arange(XW)
    table = np.zeros((KX // CELLS, 2, CELLS, 2, XW), np.float32)
    for s in range(KX // CELLS):
        cosine, sine = twiddle((s * CELLS + cell)[:, None], rows[None, :], KX)
        table[s, 0, :, 0] = cosine
        table[s, 0, :, 1] = sine
        table[s, 1, :, 0] = -sine
        table[s, 1, :, 1] = cosine
    return table.reshape(2 * KX, 2 * XW)


def line_table(length):
    index = np.arange(length)
    cosine, sine = twiddle(index[:, None], index[None, :], length)
    return np.block([[cosine, -sine], [sine, cosine]])


def depth_tables(length):
    index = np.arange(length)
    cosine, sine = twiddle(index[:, None], index[None, :], length)
    return np.stack([cosine, sine, -sine])


def grid_kernel(pos_ref, count_ref, samples_ref, out_ref, pos_s):
    tiles = STEP // 32
    sample = lax.broadcasted_iota(jnp.int32, (CELLS, STEP), 0)
    live = sample < count_ref[...]
    pos = jnp.where(live, pos_ref[...].astype(jnp.float32) * 0.4, -100.0)
    pos_s[:, 0:CELLS] = pos.T
    mids = (lax.broadcasted_iota(jnp.int32, (CELLS, 256), 0).astype(jnp.float32) + 0.5) * 0.4
    low = lax.broadcasted_iota(jnp.int32, (8, 128), 1) < 64
    sub = lax.broadcasted_iota(jnp.int32, (32, 128), 0) % 8
    lane_half = lax.broadcasted_iota(jnp.int32, (32, 128), 1) // 64
    keep = lane_half == sub % 2
    group = sub // 2

    def one_tile(t, carry):
        start = pl.multiple_of(t * 32, 32)
        pos_rows = pos_s[pl.ds(start, 32), :]
        halves = []
        for h in range(2):
            even = pos_rows[16 * h : 16 * h + 8]
            odd = pltpu.roll(pos_rows[16 * h + 8 : 16 * h + 16], 64, 1)
            halves.append(jnp.where(low, even, odd))
        row4 = jnp.concatenate(halves, axis=1)
        parts = []
        for nb in range(8):
            offset = row4[nb : nb + 1, :] - mids
            bump = jnp.maximum(1.0 - offset * offset, 0.0)
            parts.append((bump * bump).astype(jnp.bfloat16))
        weights = jnp.concatenate(parts, axis=0)
        vals = samples_ref[pl.ds(start, 32), :].astype(jnp.float32)
        zero = jnp.zeros((8, 128), jnp.float32)
        lhs = []
        for p in range(2):
            for kb in range(4):
                piece = vals[8 * kb : 8 * kb + 8]
                if kb % 2 != p:
                    piece = pltpu.roll(piece, 64, 1)
                piece = jnp.where(low == (kb % 2 == 0), piece, 0.0)
                lhs.append(jnp.concatenate([piece, zero] if kb < 2 else [zero, piece], axis=1))
        lhs = jnp.concatenate(lhs, axis=0).astype(jnp.bfloat16)
        full = lax.dot_general(lhs, weights, NT, preferred_element_type=jnp.float32)
        sides = []
        for p in range(2):
            block = full[32 * p : 32 * p + 32]
            own = jnp.where(group == 0, block[:, 0:128], block[:, 128:256])
            own = jnp.where(group == 2, block[:, 256:384], own)
            own = jnp.where(group == 3, block[:, 384:512], own)
            own = jnp.where(keep, own, 0.0)
            sides.append(own + pltpu.roll(own, 64, 1))
        out_ref[pl.ds(start, 32), :] = jnp.where(lane_half == 0, sides[0], sides[1]).astype(jnp.bfloat16)
        return carry

    lax.fori_loop(0, tiles, one_tile, 0, unroll=True)


def grid_blocks(pos_t, count, samples):
    blocks = samples.shape[0]
    return pl.pallas_call(
        grid_kernel,
        grid=(blocks // STEP,),
        in_specs=[
            pl.BlockSpec((CELLS, STEP), lambda i: (0, i)),
            pl.BlockSpec((1, STEP), lambda i: (0, i)),
            pl.BlockSpec((STEP, 128), lambda i: (i, 0)),
        ],
        out_specs=pl.BlockSpec((STEP, 128), lambda i: (i, 0)),
        out_shape=jax.ShapeDtypeStruct((blocks, 128), jnp.bfloat16),
        scratch_shapes=[pltpu.VMEM((STEP, 128), jnp.float32)],
        compiler_params=pltpu.CompilerParams(vmem_limit_bytes=60 * 1024 * 1024),
        name="grid_blocks",
    )(pos_t, count, samples)


def pack_kernel(slot_ref, row_ref, zeros_ref, values_ref, out_ref, target_ref, wide):
    pltpu.sync_copy(zeros_ref, target_ref)
    wide[...] = jnp.zeros_like(wide)

    def some(i, carry):
        start = pl.multiple_of(i * 16, 16)
        values = values_ref[pl.ds(start, 16), :].astype(jnp.float32)
        for q in range(16):
            slot = slot_ref[start + q]
            wide[pl.ds(slot, 1), :] = values[q : q + 1]
            target_ref[slot] = row_ref[start + q]
        return carry

    lax.fori_loop(0, values_ref.shape[0] // 16, some, 0, unroll=2)
    out_ref[...] = wide[...].astype(jnp.bfloat16)


def pack_rows(slot, row, values, slots):
    blocks = values.shape[0]
    return pl.pallas_call(
        pack_kernel,
        grid_spec=pltpu.PrefetchScalarGridSpec(
            num_scalar_prefetch=2,
            grid=(1,),
            in_specs=[
                pl.BlockSpec(memory_space=pl.ANY),
                pl.BlockSpec((blocks, 128), lambda i, slot, row: (0, 0)),
            ],
            out_specs=[
                pl.BlockSpec((slots, 128), lambda i, slot, row: (0, 0)),
                pl.BlockSpec(memory_space=pltpu.SMEM),
            ],
            scratch_shapes=[pltpu.VMEM((slots, 128), jnp.float32)],
        ),
        out_shape=[
            jax.ShapeDtypeStruct((slots, 128), jnp.bfloat16),
            jax.ShapeDtypeStruct((slots,), jnp.int32),
        ],
        compiler_params=pltpu.CompilerParams(vmem_limit_bytes=48 * 1024 * 1024),
        name="pack_rows",
    )(slot, row, jnp.zeros((slots,), jnp.int32), values)


def add_kernel(rows_ref, *refs):
    values_refs, table_ref, out_ref, accs = refs[:LANES], refs[LANES], refs[LANES + 1], refs[LANES + 2 :]
    segments = KX // CELLS
    step = pl.program_id(0)
    length = values_refs[0].shape[0]
    share = length * pl.num_programs(0)

    @pl.when(step == 0)
    def _():
        for acc in accs:
            acc[...] = jnp.zeros_like(acc)

    def some(i, carry):
        start = pl.multiple_of(i * 16, 16)
        values = [ref[pl.ds(start, 16), :].astype(jnp.float32) for ref in values_refs]
        for q in range(16):
            for n in range(LANES):
                row = rows_ref[n * share + step * length + start + q]
                accs[n][pl.ds(row, 1), :] += values[n][q : q + 1]
        return carry

    lax.fori_loop(0, length // 16, some, 0)

    @pl.when(step == pl.num_programs(0) - 1)
    def _():
        x_rows = None
        for n in range(segments):
            every = pl.ds(n, out_ref.shape[0], stride=segments)
            total = accs[0][every, :]
            for acc in accs[1:]:
                total = total + acc[every, :]
            kspace = total.astype(jnp.bfloat16)
            term = jnp.dot(kspace, table_ref[n], preferred_element_type=jnp.float32)
            x_rows = term if x_rows is None else x_rows + term
        out_ref[...] = x_rows.astype(jnp.bfloat16)


def add_rows(rows, values, table, total):
    slots = values.shape[0]
    steps = slots // LANES // ADDED
    return pl.pallas_call(
        add_kernel,
        grid_spec=pltpu.PrefetchScalarGridSpec(
            num_scalar_prefetch=1,
            grid=(steps,),
            in_specs=[
                pl.BlockSpec((ADDED, 128), lambda i, rows, n=n: (n * steps + i, 0)) for n in range(LANES)
            ]
            + [pl.BlockSpec(table.shape, lambda i, rows: (0, 0, 0))],
            out_specs=pl.BlockSpec((total // table.shape[0], table.shape[2]), lambda i, rows: (0, 0)),
            scratch_shapes=[pltpu.VMEM((total, 128), jnp.float32)] * LANES,
        ),
        out_shape=jax.ShapeDtypeStruct((total // table.shape[0], table.shape[2]), jnp.bfloat16),
        compiler_params=pltpu.CompilerParams(vmem_limit_bytes=58 * 1024 * 1024),
        name="add_rows",
    )(rows, *[values] * LANES, table)


def slots_of(slab, slabs, capacity):
    hot = slab[:, None] == jnp.arange(slabs, dtype=jnp.int32)[None, :]
    chunks = hot.reshape(-1, 128, slabs).astype(jnp.float32)
    inner = jnp.asarray(np.tril(np.ones((128, 128)), -1), jnp.float32)
    outer = jnp.asarray(np.tril(np.ones((chunks.shape[0], chunks.shape[0])), -1), jnp.float32)
    exact = lax.Precision.HIGHEST
    before = jnp.einsum("ij,cjs->cis", inner, chunks, precision=exact)
    before += jnp.einsum("cd,ds->cs", outer, jnp.sum(chunks, axis=1), precision=exact)[:, None]
    rank = jnp.sum(before * chunks, axis=2).reshape(-1)
    return slab * capacity + (rank + 0.5).astype(jnp.int32)


def per_device(samples, sample_pos, block_count, grid_block, block_slab, sensitivity):
    slabs = lax.axis_size("slab")
    groups = lax.axis_size("coil")
    blocks = samples.shape[1]
    planes = sensitivity.shape[1]
    coils = sensitivity.shape[0]
    width = sensitivity.shape[2]
    capacity = 5 * blocks // (2 * slabs)
    slot = slots_of(block_slab[:, 0], slabs, capacity)
    gridded = grid_blocks(sample_pos.T, block_count[None], samples[0])
    packed, target = pack_rows(slot, grid_block, gridded, slabs * capacity)
    packed = packed.reshape(slabs, capacity, 128)
    packed = lax.all_to_all(packed, "slab", split_axis=0, concat_axis=0, tiled=True)
    target = target.reshape(slabs, capacity // 128, 128)
    target = lax.all_to_all(target, "slab", split_axis=0, concat_axis=0, tiled=True)
    table = jnp.asarray(across_table().reshape(KX // CELLS, 2 * CELLS, 2 * XW), jnp.bfloat16)
    x_rows = add_rows(
        target.reshape(-1), packed.reshape(-1, 128), table, planes * KY * KX // CELLS
    )
    y_planes = jnp.einsum(
        "zkqx,qkn->zxn",
        x_rows.reshape(planes, KY, 2, XW),
        jnp.asarray(line_table(KY).T.reshape(2, KY, 2 * KY), jnp.bfloat16),
        preferred_element_type=jnp.float32,
    ).astype(jnp.bfloat16)
    lines = lax.all_to_all(y_planes, "slab", split_axis=1, concat_axis=0, tiled=True)
    lines = lines.reshape(Z, 2, KY)
    turns = jnp.asarray(depth_tables(Z), jnp.bfloat16)
    turns = jnp.stack([jnp.stack([turns[0], turns[2]]), jnp.stack([turns[1], turns[0]])])
    whole = jnp.einsum("pqzk,kqy->zpy", turns, lines, preferred_element_type=jnp.float32)
    whole = whole.astype(jnp.bfloat16).reshape(slabs, planes, 2 * KY)
    own = lax.all_to_all(whole, "slab", split_axis=0, concat_axis=0, tiled=True)
    whole, half_maps = lax.optimization_barrier((whole, sensitivity[..., :KY]))
    map_re = half_maps.astype(jnp.float32)
    own, map_re, half_maps = lax.optimization_barrier((own, map_re, sensitivity[..., KY:]))
    own = own.reshape(groups, width, planes, 2 * KY)
    own = lax.all_to_all(own, "coil", split_axis=0, concat_axis=0, tiled=True)
    own, map_im = lax.optimization_barrier((own, half_maps.astype(jnp.float32)))
    own = jnp.swapaxes(own.reshape(coils, width, planes, 2 * KY), 1, 2).astype(jnp.float32)
    img_re, img_im = own[..., :KY], own[..., KY:]
    real_part = jnp.sum(map_re * img_re + map_im * img_im, axis=0)
    imag_part = jnp.sum(map_re * img_im - map_im * img_re, axis=0)
    return jnp.concatenate([real_part, imag_part], axis=-1)


def solution(mesh):
    return jax.shard_map(
        per_device,
        mesh=mesh,
        in_specs=(
            P("coil", "slab", None),
            P("slab", None),
            P("slab"),
            P("slab"),
            P("slab", None),
            P(None, "slab", "coil", None),
        ),
        out_specs=P("slab", "coil", None),
        check_vma=False,
    )
```

```python
import functools
import math

import jax
import jax.numpy as jnp
import numpy as np
from jax import lax
from jax.experimental import pallas as pl
from jax.experimental.pallas import tpu as pltpu
from jax.sharding import PartitionSpec as P

KX = 256
KY = 256
Z = 256
XW = 16
CELLS = 64
SLABS = 16
STEP = 2048
LANES = 4
NT = (((1,), (1,)), ((), ()))


def twiddle(first, second, length):
    phase = (first * second % length).astype(np.float32) * np.float32(2.0 * math.pi / length)
    scale = 1.0 / math.sqrt(length)
    return np.cos(phase) * scale, np.sin(phase) * scale


def across_table():
    cell = np.arange(CELLS)
    rows = (KX - XW) // 2 + np.arange(XW)
    table = np.zeros((KX // CELLS, 2, CELLS, 2, XW), np.float32)
    for s in range(KX // CELLS):
        cosine, sine = twiddle((s * CELLS + cell)[:, None], rows[None, :], KX)
        table[s, 0, :, 0] = cosine
        table[s, 0, :, 1] = sine
        table[s, 1, :, 0] = -sine
        table[s, 1, :, 1] = cosine
    return table.reshape(2 * KX, 2 * XW)


def line_table(length):
    index = np.arange(length)
    cosine, sine = twiddle(index[:, None], index[None, :], length)
    return np.block([[cosine, -sine], [sine, cosine]])


def depth_tables(length):
    index = np.arange(length)
    cosine, sine = twiddle(index[:, None], index[None, :], length)
    return np.stack([cosine, sine, -sine])


def grid_kernel(pos_ref, count_ref, samples_ref, out_ref, pos_s):
    tiles = STEP // 32
    sample = lax.broadcasted_iota(jnp.int32, (CELLS, STEP), 0)
    live = sample < count_ref[...]
    pos = jnp.where(live, pos_ref[...].astype(jnp.float32) * 0.4, -100.0)
    pos_s[:, 0:CELLS] = pos.T
    mids = (lax.broadcasted_iota(jnp.int32, (CELLS, 256), 0).astype(jnp.float32) + 0.5) * 0.4
    low = lax.broadcasted_iota(jnp.int32, (8, 128), 1) < 64
    sub = lax.broadcasted_iota(jnp.int32, (32, 128), 0) % 8
    lane_half = lax.broadcasted_iota(jnp.int32, (32, 128), 1) // 64
    keep = lane_half == sub % 2
    group = sub // 2

    def one_tile(t, carry):
        start = pl.multiple_of(t * 32, 32)
        pos_rows = pos_s[pl.ds(start, 32), :]
        halves = []
        for h in range(2):
            even = pos_rows[16 * h : 16 * h + 8]
            odd = pltpu.roll(pos_rows[16 * h + 8 : 16 * h + 16], 64, 1)
            halves.append(jnp.where(low, even, odd))
        row4 = jnp.concatenate(halves, axis=1)
        parts = []
        for nb in range(8):
            offset = row4[nb : nb + 1, :] - mids
            bump = jnp.maximum(1.0 - offset * offset, 0.0)
            parts.append((bump * bump).astype(jnp.bfloat16))
        weights = jnp.concatenate(parts, axis=0)
        vals = samples_ref[pl.ds(start, 32), :].astype(jnp.float32)
        zero = jnp.zeros((8, 128), jnp.float32)
        lhs = []
        for p in range(2):
            for kb in range(4):
                piece = vals[8 * kb : 8 * kb + 8]
                if kb % 2 != p:
                    piece = pltpu.roll(piece, 64, 1)
                piece = jnp.where(low == (kb % 2 == 0), piece, 0.0)
                lhs.append(jnp.concatenate([piece, zero] if kb < 2 else [zero, piece], axis=1))
        lhs = jnp.concatenate(lhs, axis=0).astype(jnp.bfloat16)
        full = lax.dot_general(lhs, weights, NT, preferred_element_type=jnp.float32)
        sides = []
        for p in range(2):
            block = full[32 * p : 32 * p + 32]
            own = jnp.where(group == 0, block[:, 0:128], block[:, 128:256])
            own = jnp.where(group == 2, block[:, 256:384], own)
            own = jnp.where(group == 3, block[:, 384:512], own)
            own = jnp.where(keep, own, 0.0)
            sides.append(own + pltpu.roll(own, 64, 1))
        out_ref[pl.ds(start, 32), :] = jnp.where(lane_half == 0, sides[0], sides[1]).astype(jnp.bfloat16)
        return carry

    lax.fori_loop(0, tiles, one_tile, 0, unroll=True)


def grid_blocks(pos_t, count, samples):
    blocks = samples.shape[0]
    return pl.pallas_call(
        grid_kernel,
        grid=(blocks // STEP,),
        in_specs=[
            pl.BlockSpec((CELLS, STEP), lambda i: (0, i)),
            pl.BlockSpec((1, STEP), lambda i: (0, i)),
            pl.BlockSpec((STEP, 128), lambda i: (i, 0)),
        ],
        out_specs=pl.BlockSpec((STEP, 128), lambda i: (i, 0)),
        out_shape=jax.ShapeDtypeStruct((blocks, 128), jnp.bfloat16),
        scratch_shapes=[pltpu.VMEM((STEP, 128), jnp.float32)],
        compiler_params=pltpu.CompilerParams(vmem_limit_bytes=60 * 1024 * 1024),
        name="grid_blocks",
    )(pos_t, count, samples)


def pack_kernel(slot_ref, row_ref, zeros_ref, values_ref, out_ref, target_ref, wide):
    pltpu.sync_copy(zeros_ref, target_ref)
    wide[...] = jnp.zeros_like(wide)

    def some(i, carry):
        start = pl.multiple_of(i * 16, 16)
        values = values_ref[pl.ds(start, 16), :].astype(jnp.float32)
        for q in range(16):
            slot = slot_ref[start + q]
            wide[pl.ds(slot, 1), :] = values[q : q + 1]
            target_ref[slot] = row_ref[start + q]
        return carry

    lax.fori_loop(0, values_ref.shape[0] // 16, some, 0, unroll=2)
    slabs, padded, _ = out_ref.shape
    capacity = wide.shape[0] // slabs
    for k in range(slabs):
        out_ref[k, 0:capacity, :] = wide[k * capacity : (k + 1) * capacity, :].astype(jnp.bfloat16)
        out_ref[k, capacity:padded, :] = jnp.zeros((padded - capacity, 128), jnp.bfloat16)


def pack_rows(slot, row, values, slabs, capacity, padded):
    slots = slabs * capacity
    blocks = values.shape[0]
    return pl.pallas_call(
        pack_kernel,
        grid_spec=pltpu.PrefetchScalarGridSpec(
            num_scalar_prefetch=2,
            grid=(1,),
            in_specs=[
                pl.BlockSpec(memory_space=pl.ANY),
                pl.BlockSpec((blocks, 128), lambda i, slot, row: (0, 0)),
            ],
            out_specs=[
                pl.BlockSpec((slabs, padded, 128), lambda i, slot, row: (0, 0, 0)),
                pl.BlockSpec(memory_space=pltpu.SMEM),
            ],
            scratch_shapes=[pltpu.VMEM((slots, 128), jnp.float32)],
        ),
        out_shape=[
            jax.ShapeDtypeStruct((slabs, padded, 128), jnp.bfloat16),
            jax.ShapeDtypeStruct((slots,), jnp.int32),
        ],
        compiler_params=pltpu.CompilerParams(vmem_limit_bytes=48 * 1024 * 1024),
        name="pack_rows",
    )(slot, row, jnp.zeros((slots,), jnp.int32), values)


def add_kernel(rows_ref, *refs):
    values_refs, table_ref, out_ref, accs = refs[:LANES], refs[LANES], refs[LANES + 1], refs[LANES + 2 :]
    segments = KX // CELLS
    step = pl.program_id(0)
    length = values_refs[0].shape[1]
    share = length * pl.num_programs(0)

    @pl.when(step == 0)
    def _():
        for acc in accs:
            acc[...] = jnp.zeros_like(acc)

    def some(i, carry):
        start = pl.multiple_of(i * 16, 16)
        values = [ref[0, pl.ds(start, 16), :].astype(jnp.float32) for ref in values_refs]
        for q in range(16):
            for n in range(LANES):
                row = rows_ref[n * share + step * length + start + q]
                accs[n][pl.ds(row, 1), :] += values[n][q : q + 1]
        return carry

    lax.fori_loop(0, length // 16, some, 0)

    @pl.when(step == pl.num_programs(0) - 1)
    def _():
        x_rows = None
        for n in range(segments):
            every = pl.ds(n, out_ref.shape[0], stride=segments)
            total = accs[0][every, :]
            for acc in accs[1:]:
                total = total + acc[every, :]
            kspace = total.astype(jnp.bfloat16)
            term = jnp.dot(kspace, table_ref[n], preferred_element_type=jnp.float32)
            x_rows = term if x_rows is None else x_rows + term
        out_ref[...] = x_rows.astype(jnp.bfloat16)


def add_rows(rows, values, table, total):
    steps = values.shape[0] // LANES
    length = rows.shape[0] // values.shape[0]
    return pl.pallas_call(
        add_kernel,
        grid_spec=pltpu.PrefetchScalarGridSpec(
            num_scalar_prefetch=1,
            grid=(steps,),
            in_specs=[
                pl.BlockSpec((1, length, 128), lambda i, rows, n=n: (n * steps + i, 0, 0)) for n in range(LANES)
            ]
            + [pl.BlockSpec(table.shape, lambda i, rows: (0, 0, 0))],
            out_specs=pl.BlockSpec((total // table.shape[0], table.shape[2]), lambda i, rows: (0, 0)),
            scratch_shapes=[pltpu.VMEM((total, 128), jnp.float32)] * LANES,
        ),
        out_shape=jax.ShapeDtypeStruct((total // table.shape[0], table.shape[2]), jnp.bfloat16),
        compiler_params=pltpu.CompilerParams(vmem_limit_bytes=58 * 1024 * 1024),
        name="add_rows",
    )(rows, *[values] * LANES, table)


def slots_of(slab, slabs, capacity):
    hot = slab[:, None] == jnp.arange(slabs, dtype=jnp.int32)[None, :]
    chunks = hot.reshape(-1, 128, slabs).astype(jnp.float32)
    inner = jnp.asarray(np.tril(np.ones((128, 128)), -1), jnp.float32)
    outer = jnp.asarray(np.tril(np.ones((chunks.shape[0], chunks.shape[0])), -1), jnp.float32)
    exact = lax.Precision.HIGHEST
    before = jnp.einsum("ij,cjs->cis", inner, chunks, precision=exact)
    before += jnp.einsum("cd,ds->cs", outer, jnp.sum(chunks, axis=1), precision=exact)[:, None]
    rank = jnp.sum(before * chunks, axis=2).reshape(-1)
    return slab * capacity + (rank + 0.5).astype(jnp.int32)


def per_device(samples, sample_pos, block_count, grid_block, block_slab, sensitivity):
    slabs = lax.axis_size("slab")
    groups = lax.axis_size("coil")
    blocks = samples.shape[1]
    planes = sensitivity.shape[1]
    coils = sensitivity.shape[0]
    width = sensitivity.shape[2]
    capacity = 5 * blocks // (2 * slabs)
    slot = slots_of(block_slab[:, 0], slabs, capacity)
    gridded = grid_blocks(sample_pos.T, block_count[None], samples[0])
    spare = 16 - 2 * (capacity // 128) % 16
    padded = capacity + 2 * (capacity // 128) + spare
    packed, target = pack_rows(slot, grid_block, gridded, slabs, capacity, padded)
    target = target.reshape(slabs, capacity // 128, 128)
    marks = [target // 128, target % 128, jnp.zeros((slabs, spare, 128), jnp.int32)]
    marks = jnp.concatenate(marks, axis=1).astype(jnp.bfloat16)
    packed = lax.dynamic_update_slice(packed, marks, (0, capacity, 0))
    packed = lax.all_to_all(packed, "slab", split_axis=0, concat_axis=0, tiled=True)
    marks = packed[:, capacity : capacity + 2 * (capacity // 128)].astype(jnp.int32)
    target = marks[:, : capacity // 128] * 128 + marks[:, capacity // 128 :]
    table = jnp.asarray(across_table().reshape(KX // CELLS, 2 * CELLS, 2 * XW), jnp.bfloat16)
    x_rows = add_rows(
        target.reshape(-1), packed, table, planes * KY * KX // CELLS
    )
    y_planes = jnp.einsum(
        "zkqx,qkn->zxn",
        x_rows.reshape(planes, KY, 2, XW),
        jnp.asarray(line_table(KY).T.reshape(2, KY, 2 * KY), jnp.bfloat16),
        preferred_element_type=jnp.float32,
    ).astype(jnp.bfloat16)
    lines = lax.all_to_all(y_planes, "slab", split_axis=1, concat_axis=0, tiled=True)
    lines = lines.reshape(Z, 2, KY)
    turns = jnp.asarray(depth_tables(Z), jnp.bfloat16)
    turns = jnp.stack([jnp.stack([turns[0], turns[2]]), jnp.stack([turns[1], turns[0]])])
    whole = jnp.einsum("pqzk,kqy->zpy", turns, lines, preferred_element_type=jnp.float32)
    whole = whole.astype(jnp.bfloat16).reshape(slabs, planes, 2 * KY)
    own = lax.all_to_all(whole, "slab", split_axis=0, concat_axis=0, tiled=True)
    whole, half_maps = lax.optimization_barrier((whole, sensitivity[..., :KY]))
    map_re = half_maps.astype(jnp.float32)
    own, map_re, half_maps = lax.optimization_barrier((own, map_re, sensitivity[..., KY:]))
    own = own.reshape(groups, width, planes, 2 * KY)
    own = lax.all_to_all(own, "coil", split_axis=0, concat_axis=0, tiled=True)
    own, map_im = lax.optimization_barrier((own, half_maps.astype(jnp.float32)))
    own = jnp.swapaxes(own.reshape(coils, width, planes, 2 * KY), 1, 2).astype(jnp.float32)
    img_re, img_im = own[..., :KY], own[..., KY:]
    real_part = jnp.sum(map_re * img_re + map_im * img_im, axis=0)
    imag_part = jnp.sum(map_re * img_im - map_im * img_re, axis=0)
    return jnp.concatenate([real_part, imag_part], axis=-1)


def solution(mesh):
    return jax.shard_map(
        per_device,
        mesh=mesh,
        in_specs=(
            P("coil", "slab", None),
            P("slab", None),
            P("slab"),
            P("slab"),
            P("slab", None),
            P(None, "slab", "coil", None),
        ),
        out_specs=P("slab", "coil", None),
        check_vma=False,
    )
```

```python
import functools
import math

import jax
import jax.numpy as jnp
import numpy as np
from jax import lax
from jax.experimental import pallas as pl
from jax.experimental.pallas import tpu as pltpu
from jax.sharding import PartitionSpec as P

KX = 256
KY = 256
Z = 256
XW = 16
CELLS = 64
SLABS = 16
STEP = 2048
LANES = 4
NT = (((1,), (1,)), ((), ()))


def twiddle(first, second, length):
    phase = (first * second % length).astype(np.float32) * np.float32(2.0 * math.pi / length)
    scale = 1.0 / math.sqrt(length)
    return np.cos(phase) * scale, np.sin(phase) * scale


def across_table():
    cell = np.arange(CELLS)
    rows = (KX - XW) // 2 + np.arange(XW)
    table = np.zeros((KX // CELLS, 2, CELLS, 2, XW), np.float32)
    for s in range(KX // CELLS):
        cosine, sine = twiddle((s * CELLS + cell)[:, None], rows[None, :], KX)
        table[s, 0, :, 0] = cosine
        table[s, 0, :, 1] = sine
        table[s, 1, :, 0] = -sine
        table[s, 1, :, 1] = cosine
    return table.reshape(2 * KX, 2 * XW)


def line_table(length):
    index = np.arange(length)
    cosine, sine = twiddle(index[:, None], index[None, :], length)
    return np.block([[cosine, -sine], [sine, cosine]])


def depth_tables(length):
    index = np.arange(length)
    cosine, sine = twiddle(index[:, None], index[None, :], length)
    return np.stack([cosine, sine, -sine])


def grid_kernel(pos_ref, count_ref, samples_ref, out_ref, pos_s):
    tiles = STEP // 32
    sample = lax.broadcasted_iota(jnp.int32, (CELLS, STEP), 0)
    live = sample < count_ref[...]
    pos = jnp.where(live, pos_ref[...].astype(jnp.float32) * 0.4, -100.0)
    pos_s[:, 0:CELLS] = pos.T
    mids = (lax.broadcasted_iota(jnp.int32, (CELLS, 256), 0).astype(jnp.float32) + 0.5) * 0.4
    low = lax.broadcasted_iota(jnp.int32, (8, 128), 1) < 64
    sub = lax.broadcasted_iota(jnp.int32, (32, 128), 0) % 8
    lane_half = lax.broadcasted_iota(jnp.int32, (32, 128), 1) // 64
    keep = lane_half == sub % 2
    group = sub // 2

    def one_tile(t, carry):
        start = pl.multiple_of(t * 32, 32)
        pos_rows = pos_s[pl.ds(start, 32), :]
        halves = []
        for h in range(2):
            even = pos_rows[16 * h : 16 * h + 8]
            odd = pltpu.roll(pos_rows[16 * h + 8 : 16 * h + 16], 64, 1)
            halves.append(jnp.where(low, even, odd))
        row4 = jnp.concatenate(halves, axis=1)
        parts = []
        for nb in range(8):
            offset = row4[nb : nb + 1, :] - mids
            bump = jnp.maximum(1.0 - offset * offset, 0.0)
            parts.append((bump * bump).astype(jnp.bfloat16))
        weights = jnp.concatenate(parts, axis=0)
        vals = samples_ref[pl.ds(start, 32), :].astype(jnp.float32)
        zero = jnp.zeros((8, 128), jnp.float32)
        lhs = []
        for p in range(2):
            for kb in range(4):
                piece = vals[8 * kb : 8 * kb + 8]
                if kb % 2 != p:
                    piece = pltpu.roll(piece, 64, 1)
                piece = jnp.where(low == (kb % 2 == 0), piece, 0.0)
                lhs.append(jnp.concatenate([piece, zero] if kb < 2 else [zero, piece], axis=1))
        lhs = jnp.concatenate(lhs, axis=0).astype(jnp.bfloat16)
        full = lax.dot_general(lhs, weights, NT, preferred_element_type=jnp.float32)
        sides = []
        for p in range(2):
            block = full[32 * p : 32 * p + 32]
            own = jnp.where(group == 0, block[:, 0:128], block[:, 128:256])
            own = jnp.where(group == 2, block[:, 256:384], own)
            own = jnp.where(group == 3, block[:, 384:512], own)
            own = jnp.where(keep, own, 0.0)
            sides.append(own + pltpu.roll(own, 64, 1))
        out_ref[pl.ds(start, 32), :] = jnp.where(lane_half == 0, sides[0], sides[1]).astype(jnp.bfloat16)
        return carry

    lax.fori_loop(0, tiles, one_tile, 0, unroll=True)


def grid_blocks(pos_t, count, samples):
    blocks = samples.shape[0]
    return pl.pallas_call(
        grid_kernel,
        grid=(blocks // STEP,),
        in_specs=[
            pl.BlockSpec((CELLS, STEP), lambda i: (0, i)),
            pl.BlockSpec((1, STEP), lambda i: (0, i)),
            pl.BlockSpec((STEP, 128), lambda i: (i, 0)),
        ],
        out_specs=pl.BlockSpec((STEP, 128), lambda i: (i, 0)),
        out_shape=jax.ShapeDtypeStruct((blocks, 128), jnp.bfloat16),
        scratch_shapes=[pltpu.VMEM((STEP, 128), jnp.float32)],
        compiler_params=pltpu.CompilerParams(vmem_limit_bytes=60 * 1024 * 1024),
        name="grid_blocks",
    )(pos_t, count, samples)


def pack_kernel(slot_ref, row_ref, zeros_ref, values_ref, out_ref, target_ref, wide):
    pltpu.sync_copy(zeros_ref, target_ref)
    wide[...] = jnp.zeros_like(wide)

    def some(i, carry):
        start = pl.multiple_of(i * 16, 16)
        values = values_ref[pl.ds(start, 16), :].astype(jnp.float32)
        for q in range(16):
            slot = slot_ref[start + q]
            wide[pl.ds(slot, 1), :] = values[q : q + 1]
            target_ref[slot] = row_ref[start + q]
        return carry

    lax.fori_loop(0, values_ref.shape[0] // 16, some, 0, unroll=2)
    slabs, padded, _ = out_ref.shape
    capacity = wide.shape[0] // slabs
    for k in range(slabs):
        out_ref[k, 0:capacity, :] = wide[k * capacity : (k + 1) * capacity, :].astype(jnp.bfloat16)
        out_ref[k, capacity:padded, :] = jnp.zeros((padded - capacity, 128), jnp.bfloat16)


def pack_rows(slot, row, values, slabs, capacity, padded):
    slots = slabs * capacity
    blocks = values.shape[0]
    return pl.pallas_call(
        pack_kernel,
        grid_spec=pltpu.PrefetchScalarGridSpec(
            num_scalar_prefetch=2,
            grid=(1,),
            in_specs=[
                pl.BlockSpec(memory_space=pl.ANY),
                pl.BlockSpec((blocks, 128), lambda i, slot, row: (0, 0)),
            ],
            out_specs=[
                pl.BlockSpec((slabs, padded, 128), lambda i, slot, row: (0, 0, 0)),
                pl.BlockSpec(memory_space=pltpu.SMEM),
            ],
            scratch_shapes=[pltpu.VMEM((slots, 128), jnp.float32)],
        ),
        out_shape=[
            jax.ShapeDtypeStruct((slabs, padded, 128), jnp.bfloat16),
            jax.ShapeDtypeStruct((slots,), jnp.int32),
        ],
        compiler_params=pltpu.CompilerParams(vmem_limit_bytes=48 * 1024 * 1024),
        name="pack_rows",
    )(slot, row, jnp.zeros((slots,), jnp.int32), values)


def add_kernel(rows_ref, *refs):
    values_refs, table_ref, out_ref, accs = refs[:LANES], refs[LANES], refs[LANES + 1], refs[LANES + 2 :]
    segments = KX // CELLS
    step = pl.program_id(0)
    length = values_refs[0].shape[1]
    share = length * pl.num_programs(0)

    @pl.when(step == 0)
    def _():
        for acc in accs:
            acc[...] = jnp.zeros_like(acc)

    def some(i, carry):
        start = pl.multiple_of(i * 16, 16)
        values = [ref[0, pl.ds(start, 16), :].astype(jnp.float32) for ref in values_refs]
        for q in range(16):
            for n in range(LANES):
                row = rows_ref[n * share + step * length + start + q]
                accs[n][pl.ds(row, 1), :] += values[n][q : q + 1]
        return carry

    lax.fori_loop(0, length // 16, some, 0)

    @pl.when(step == pl.num_programs(0) - 1)
    def _():
        x_rows = None
        for n in range(segments):
            every = pl.ds(n, out_ref.shape[0], stride=segments)
            total = accs[0][every, :]
            for acc in accs[1:]:
                total = total + acc[every, :]
            kspace = total.astype(jnp.bfloat16)
            term = jnp.dot(kspace, table_ref[n], preferred_element_type=jnp.float32)
            x_rows = term if x_rows is None else x_rows + term
        out_ref[...] = x_rows.astype(jnp.bfloat16)


def add_rows(rows, values, table, total):
    steps = values.shape[0] // LANES
    length = rows.shape[0] // values.shape[0]
    return pl.pallas_call(
        add_kernel,
        grid_spec=pltpu.PrefetchScalarGridSpec(
            num_scalar_prefetch=1,
            grid=(steps,),
            in_specs=[
                pl.BlockSpec((1, length, 128), lambda i, rows, n=n: (n * steps + i, 0, 0)) for n in range(LANES)
            ]
            + [pl.BlockSpec(table.shape, lambda i, rows: (0, 0, 0))],
            out_specs=pl.BlockSpec((total // table.shape[0], table.shape[2]), lambda i, rows: (0, 0)),
            scratch_shapes=[pltpu.VMEM((total, 128), jnp.float32)] * LANES,
        ),
        out_shape=jax.ShapeDtypeStruct((total // table.shape[0], table.shape[2]), jnp.bfloat16),
        compiler_params=pltpu.CompilerParams(vmem_limit_bytes=42 * 1024 * 1024),
        name="add_rows",
    )(rows, *[values] * LANES, table)


def slots_of(slab, slabs, capacity):
    hot = slab[:, None] == jnp.arange(slabs, dtype=jnp.int32)[None, :]
    chunks = hot.reshape(-1, 128, slabs).astype(jnp.float32)
    inner = jnp.asarray(np.tril(np.ones((128, 128)), -1), jnp.float32)
    outer = jnp.asarray(np.tril(np.ones((chunks.shape[0], chunks.shape[0])), -1), jnp.float32)
    exact = lax.Precision.HIGHEST
    before = jnp.einsum("ij,cjs->cis", inner, chunks, precision=exact)
    before += jnp.einsum("cd,ds->cs", outer, jnp.sum(chunks, axis=1), precision=exact)[:, None]
    rank = jnp.sum(before * chunks, axis=2).reshape(-1)
    return slab * capacity + (rank + 0.5).astype(jnp.int32)


def per_device(samples, sample_pos, block_count, grid_block, block_slab, sensitivity):
    slabs = lax.axis_size("slab")
    groups = lax.axis_size("coil")
    blocks = samples.shape[1]
    planes = sensitivity.shape[1]
    coils = sensitivity.shape[0]
    width = sensitivity.shape[2]
    capacity = 5 * blocks // (2 * slabs)
    slot = slots_of(block_slab[:, 0], slabs, capacity)
    gridded = grid_blocks(sample_pos.T, block_count[None], samples[0])
    spare = 16 - 2 * (capacity // 128) % 16
    padded = capacity + 2 * (capacity // 128) + spare
    packed, target = pack_rows(slot, grid_block, gridded, slabs, capacity, padded)
    target = target.reshape(slabs, capacity // 128, 128)
    marks = [target // 128, target % 128, jnp.zeros((slabs, spare, 128), jnp.int32)]
    marks = jnp.concatenate(marks, axis=1).astype(jnp.bfloat16)
    packed = lax.dynamic_update_slice(packed, marks, (0, capacity, 0))
    packed = lax.all_to_all(packed, "slab", split_axis=0, concat_axis=0, tiled=True)
    marks = packed[:, capacity : capacity + 2 * (capacity // 128)].astype(jnp.int32)
    target = marks[:, : capacity // 128] * 128 + marks[:, capacity // 128 :]
    table = jnp.asarray(across_table().reshape(KX // CELLS, 2 * CELLS, 2 * XW), jnp.bfloat16)
    x_rows = add_rows(
        target.reshape(-1), packed, table, planes * KY * KX // CELLS
    )
    y_planes = jnp.einsum(
        "zkqx,qkn->zxn",
        x_rows.reshape(planes, KY, 2, XW),
        jnp.asarray(line_table(KY).T.reshape(2, KY, 2 * KY), jnp.bfloat16),
        preferred_element_type=jnp.float32,
    ).astype(jnp.bfloat16)
    lines = lax.all_to_all(y_planes, "slab", split_axis=1, concat_axis=0, tiled=True)
    lines = lines.reshape(Z, 2, KY)
    turns = jnp.asarray(depth_tables(Z), jnp.bfloat16)
    turns = jnp.stack([jnp.stack([turns[0], turns[2]]), jnp.stack([turns[1], turns[0]])])
    whole = jnp.einsum("pqzk,kqy->zpy", turns, lines, preferred_element_type=jnp.float32)
    whole = whole.astype(jnp.bfloat16).reshape(slabs, planes, 2 * KY)
    own = lax.all_to_all(whole, "slab", split_axis=0, concat_axis=0, tiled=True)
    whole, half_maps = lax.optimization_barrier((whole, sensitivity[..., :KY]))
    map_re = half_maps.astype(jnp.float32)
    own, map_re, half_maps = lax.optimization_barrier((own, map_re, sensitivity[..., KY:]))
    own = own.reshape(groups, width, planes, 2 * KY)
    own = lax.all_to_all(own, "coil", split_axis=0, concat_axis=0, tiled=True)
    own, map_im = lax.optimization_barrier((own, half_maps.astype(jnp.float32)))
    own = jnp.swapaxes(own.reshape(coils, width, planes, 2 * KY), 1, 2).astype(jnp.float32)
    img_re, img_im = own[..., :KY], own[..., KY:]
    real_part = jnp.sum(map_re * img_re + map_im * img_im, axis=0)
    imag_part = jnp.sum(map_re * img_im - map_im * img_re, axis=0)
    return jnp.concatenate([real_part, imag_part], axis=-1)


def solution(mesh):
    return jax.shard_map(
        per_device,
        mesh=mesh,
        in_specs=(
            P("coil", "slab", None),
            P("slab", None),
            P("slab"),
            P("slab"),
            P("slab", None),
            P(None, "slab", "coil", None),
        ),
        out_specs=P("slab", "coil", None),
        check_vma=False,
    )
```
